32 devices in a mesh: grp: 4 (over y, core), brick: 8 (over z, x).
Axes of the slice: x: 2, y: 2, z: 4, core: 2. Of those that a mesh axis runs over, the one named last changes fastest.
Arguments:
- right_side: float32 [3, 64, 128, 128], P(None, 'grp', 'brick'), may hold values from -24 to 24
- stiffness: float32 [64, 128, 128], P('grp', 'brick'), may hold values from 1 to 10
- reaction: float32 [64, 128, 128], P('grp', 'brick'), may hold values from 0.1 to 1
Outputs:
- correction: float32 [3, 64, 128, 128], P(None, 'grp', 'brick')
The draws below stay inside these ranges and needn't reach their ends.
All inputs are finite; a program needn't handle non-finite values.
Results may differ from the reference program's by a relative error of at most 0.00025.
Values sent between devices are 32-bit elements; how exact they have to be, the bound alone decides.
A program may use at most 128 MiB of HBM per device.

```python
import math
import jax
import jax.numpy as jnp

NZ = 128
LEVELS = 4
NX = 64
NY = 128


def draw_right_side(key, part):
    key = jax.random.fold_in(key, 11)
    return 6.0 * jax.random.truncated_normal(key, -4.0, 4.0, (3, NX, NY, NZ), jnp.float32)


def level_of(rng, shape, shards, low, largest):
    loudness = 1.0
    for dim, blocks in shards:
        draws = jax.random.uniform(jax.random.fold_in(jax.random.fold_in(rng, 6), dim), (blocks,), jnp.float32, low / len(shards), largest / len(shards))
        loudness = loudness * jnp.repeat(jnp.exp(draws), shape[dim] // blocks).reshape((-1,) + (1,) * (len(shape) - 1 - dim))
    return loudness


def setup_inputs(seed: int = 0) -> dict:
    key_of = jax.random.split(jax.random.key(seed), 4)
    right_side = draw_right_side(jax.random.fold_in(key_of[3], 71), 0)
    stiffness = jnp.clip(jnp.exp(math.log(10.0) - 2.3025851 * jax.random.uniform(key_of[1], (NX, NY, NZ), jnp.float32) ** level_of(key_of[1], (NX, NY, NZ), ((0, 4), (1, 8)), -0.2, 0.2)), 1.0, 10.0)
    reaction = jnp.clip(jnp.exp(math.log(1.0) - 2.3025851 * jax.random.uniform(key_of[2], (NX, NY, NZ), jnp.float32) ** level_of(key_of[2], (NX, NY, NZ), ((0, 4), (1, 8)), -0.2, 0.2)), 0.1, 1.0)
    return dict(right_side=right_side, stiffness=stiffness, reaction=reaction)


BETA = 1.0
THETA = 1.5
DELTA = 1.0
SIGMA = 1.5


def rate_list():
    rates = [1.0 / SIGMA]
    for number in range(3):
        rates.append(1.0 / (2.0 * SIGMA - rates[-1]))
    return rates


def advance(step, old, resid, inverse):
    rates = rate_list()
    return rates[step] * rates[step - 1] * old + (2.0 * rates[step] / DELTA) * (inverse * resid)


def offset_of(axis, sign):
    return tuple(sign if index == axis else 0 for index in range(3))


def view(array, shift, rows, cols, depth):
    return array[..., 1 + shift[0]:1 + shift[0] + rows, 1 + shift[1]:1 + shift[1] + cols, 1 + shift[2]:1 + shift[2] + depth]


def face_total(stiff, rows, cols, depth):
    centre = view(stiff, (0, 0, 0), rows, cols, depth)
    total = jnp.zeros_like(centre)
    for axis in range(3):
        total = total + 0.5 * (centre + view(stiff, offset_of(axis, 1), rows, cols, depth))
        total = total + 0.5 * (centre + view(stiff, offset_of(axis, -1), rows, cols, depth))
    return total


def inverse_diagonal(coeff, scale):
    rows = coeff.shape[1] - 2
    cols = coeff.shape[2] - 2
    depth = coeff.shape[3]
    stiff = jnp.pad(coeff[0], ((0, 0), (0, 0), (1, 1)))
    react = coeff[1, 1:-1, 1:-1, :]
    faces = face_total(stiff, rows, cols, depth)
    return (1.0 / (scale * (faces + 2.0 * BETA) + react))[None]


def operate(field, coeff, scale):
    rows = field.shape[1] - 2
    cols = field.shape[2] - 2
    depth = field.shape[3]
    padded = jnp.pad(field, ((0, 0), (0, 0), (0, 0), (1, 1)))
    stiff = jnp.pad(coeff[0], ((0, 0), (0, 0), (1, 1)))
    react = coeff[1, 1:-1, 1:-1, :]
    centre = view(stiff, (0, 0, 0), rows, cols, depth)
    middle = view(padded, (0, 0, 0), rows, cols, depth)
    laplace = jnp.zeros_like(middle)
    for axis in range(3):
        ahead = offset_of(axis, 1)
        behind = offset_of(axis, -1)
        upper = 0.5 * (centre + view(stiff, ahead, rows, cols, depth))
        lower = 0.5 * (centre + view(stiff, behind, rows, cols, depth))
        laplace = laplace + upper * (middle - view(padded, ahead, rows, cols, depth))
        laplace = laplace + lower * (middle - view(padded, behind, rows, cols, depth))

    def divergence(anchor):
        total = jnp.zeros_like(centre)
        for axis in range(3):
            moved = tuple(anchor[index] + offset_of(axis, 1)[index] for index in range(3))
            total = total + view(padded[axis], moved, rows, cols, depth) - view(padded[axis], anchor, rows, cols, depth)
        return total

    centre_div = divergence((0, 0, 0))
    parts = []
    for axis in range(3):
        graddiv = divergence(offset_of(axis, -1)) - centre_div
        parts.append(scale * (laplace[axis] + BETA * graddiv) + react * middle[axis])
    return jnp.stack(parts)


def shrink(array):
    comps, rows, cols, depth = array.shape
    blocks = array.reshape(comps, rows // 2, 2, cols // 2, 2, depth // 2, 2)
    return blocks.mean(axis=(2, 4, 6))


def grow(array):
    return jnp.repeat(jnp.repeat(jnp.repeat(array, 2, axis=1), 2, axis=2), 2, axis=3)


def widen(array, width):
    return jnp.pad(array, ((0, 0), (width, width), (width, width), (0, 0)))


def reference(right_side, stiffness, reaction):
    coeff = jnp.stack([stiffness, reaction])
    levels = []
    for level in range(LEVELS):
        if level > 0:
            coeff = shrink(coeff)
        padded = widen(coeff, 1)
        scale = 0.25 ** level
        levels.append((padded, inverse_diagonal(padded, scale), scale))

    def product(field, level):
        padded, inverse, scale = levels[level]
        return operate(widen(field, 1), padded, scale)

    def relax(source, start, level):
        inverse = levels[level][1]
        if start is None:
            resid = source
            state = jnp.zeros_like(source)
        else:
            resid = source - product(start, level)
            state = start
        step_dir = inverse * resid / THETA
        for step in range(1, 4):
            state = state + step_dir
            resid = source - product(state, level)
            step_dir = advance(step, step_dir, resid, inverse)
        return state + step_dir

    sources = [right_side]
    saved = []
    for level in range(LEVELS - 1):
        smooth = relax(sources[level], None, level)
        saved.append(smooth)
        resid = sources[level] - product(smooth, level)
        sources.append(shrink(resid))
    answer = relax(sources[-1], None, LEVELS - 1)
    for level in reversed(range(LEVELS - 1)):
        answer = relax(sources[level], saved[level] + grow(answer), level)
    return answer
```

```python
import jax
import jax.numpy as jnp
from jax import lax
from jax.experimental import pallas as pl
from jax.experimental.pallas import tpu as pltpu
from jax.sharding import PartitionSpec as P

BETA = 1.0
THETA = 1.5
DELTA = 1.0
SIGMA = 1.5
HX = 6
HY = 8
LANES = 128
DIRS = [(a, b) for a in (-1, 0, 1) for b in (-1, 0, 1) if (a, b) != (0, 0)]


def rate_list():
    rates = [1.0 / SIGMA]
    for number in range(3):
        rates.append(1.0 / (2.0 * SIGMA - rates[-1]))
    return rates


def round8(number):
    return -(-number // 8) * 8


def lane(rows):
    return lax.broadcasted_iota(jnp.int32, (rows, LANES), 1)


def roll(value, shift):
    return pltpu.roll(value, shift % LANES, 1)


def pack(values, group):
    if group == 1:
        return values[0]
    place = lane(values[0].shape[0]) % group
    out = values[0]
    for t in range(1, len(values)):
        out = jnp.where(place == t, values[t], out)
    return out


def unpack(value, group, t):
    if group == 1:
        return value
    out = jnp.where(lane(value.shape[0]) % group == t, value, 0.0)
    if t:
        out = roll(out, -t)
    shift = 1
    while shift < group:
        out = out + roll(out, shift)
        shift *= 2
    return out


def halve_lanes(value, group):
    first = lane(value.shape[0]) % (2 * group) < group
    return value + jnp.where(first, roll(value, -group), roll(value, group))


class Exchange:
    def __init__(self, size, group, packed, widths):
        self.size, self.group, self.packed, self.widths = size, group, packed, widths
        self.blocks = size // group
        self.offs = [sum(widths[:n]) for n in range(len(widths))]
        self.rows = round8(sum(widths))
        self.xrows = round8(len(widths) * size)

    def scratch(self):
        f32 = jnp.float32
        return [
            pltpu.VMEM((2, self.packed, self.xrows, LANES), f32),
            pltpu.VMEM((2, self.blocks, self.rows, LANES), f32),
            pltpu.VMEM((2, self.packed, self.xrows, LANES), f32),
            pltpu.VMEM((2, self.blocks + 2 * self.packed, self.rows, LANES), f32),
            pltpu.SemaphoreType.DMA((8,)),
            pltpu.SemaphoreType.DMA((8,)),
        ]

    def bind(self, refs, where):
        self.sx, self.sy, self.rx, self.ry, self.ssem, self.rsem = refs
        self.where = where

    def copy(self, ex, ey):
        g, b, _ = self.where
        n, w = self.blocks, self.packed
        if ey == 0:
            side = 0 if ex < 0 else 1
            src, dst = self.sx.at[side], self.rx.at[1 - side]
        else:
            side = 0 if ey < 0 else 1
            src, dst = self.sy.at[side], self.ry.at[1 - side]
            if ex == 0:
                dst = dst.at[pl.ds(w, n)]
            elif ex < 0:
                src, dst = src.at[pl.ds(0, w)], dst.at[pl.ds(w + n, w)]
            else:
                src, dst = src.at[pl.ds(n - w, w)], dst.at[pl.ds(0, w)]
        return pltpu.make_async_remote_copy(
            src_ref=src,
            dst_ref=dst,
            send_sem=self.ssem.at[DIRS.index((ex, ey))],
            recv_sem=self.rsem.at[DIRS.index((-ex, -ey))],
            device_id=(g + ex, b + ey),
            device_id_type=pl.DeviceIdType.MESH,
        )

    def stage(self, get):
        def put(j, field, r0, count, ref, side, row, off):
            values = [get(field, j * self.group + t, r0, count) for t in range(self.group)]
            ref[side, row, off : off + count, :] = pack(values, self.group)

        def body(j, carry):
            for field, width in enumerate(self.widths):
                for side in (0, 1):
                    r0 = 0 if side == 0 else self.size - width
                    put(j, field, r0, width, self.sy, side, j, self.offs[field])
            return carry

        if self.blocks > 4:
            lax.fori_loop(0, self.blocks, body, 0)
        else:
            for j in range(self.blocks):
                body(j, 0)
        for side in (0, 1):
            for j in range(self.packed):
                for field in range(len(self.widths)):
                    at = j if side == 0 else self.blocks - self.packed + j
                    put(at, field, 0, self.size, self.sx, side, j, field * self.size)

    def start(self):
        exists = self.where[2]
        for d in DIRS:
            @pl.when(exists[d])
            def _(d=d):
                self.copy(*d).start()

    def finish_send(self):
        exists = self.where[2]
        for d in DIRS:
            @pl.when(exists[d])
            def _(d=d):
                self.copy(*d).wait_send()

    def finish(self, put):
        exists = self.where[2]
        size, group = self.size, self.group

        def spread_rows(ref, side, row, x0, off, field, y0, count):
            value = ref[side, row, off : off + count, :]
            for t in range(group):
                put(field, x0 + t, y0, unpack(value, group, t))

        for d in DIRS:
            @pl.when(exists[d])
            def _(d=d):
                dx, dy = d
                self.copy(-dx, -dy).wait_recv()
                if dy == 0:
                    side = 0 if dx < 0 else 1
                    base = -self.packed * group if dx < 0 else size
                    for j in range(self.packed):
                        for field in range(len(self.widths)):
                            spread_rows(
                                self.rx, side, j, base + j * group, field * size, field, 0, size
                            )
                    return
                side = 0 if dy < 0 else 1
                first, count = {
                    -1: (0, self.packed),
                    0: (self.packed, self.blocks),
                    1: (self.packed + self.blocks, self.packed),
                }[dx]

                def body(j, carry):
                    for field, width in enumerate(self.widths):
                        y0 = -width if dy < 0 else size
                        spread_rows(
                            self.ry,
                            side,
                            first + j,
                            (first + j - self.packed) * group,
                            self.offs[field],
                            field,
                            y0,
                            width,
                        )
                    return carry

                if count > 4:
                    lax.fori_loop(0, count, body, 0)
                else:
                    for j in range(count):
                        body(j, 0)


class Level:
    NAMES = ("f", "xa", "xb", "p")
    COEFF = ("k", "rea", "kx", "ky", "kz", "kzm", "dg", "inv")

    def __init__(self, number, xsize, ysize, window):
        self.number, self.xsize, self.ysize, self.window = number, xsize, ysize, window
        self.group = 2**number
        self.scale = 0.25**number
        self.shape = (xsize + 2 * HX, round8(ysize) + 2 * HY, LANES)

    def scratch(self):
        f32 = jnp.float32
        return [pltpu.VMEM((3,) + self.shape, f32) for _ in self.NAMES] + [
            pltpu.VMEM(self.shape, f32) for _ in self.COEFF
        ]

    def bind(self, refs):
        for name, ref in zip(self.NAMES + self.COEFF, refs):
            setattr(self, name, ref)

    def clear(self):
        zero = jnp.zeros(self.shape[1:], jnp.float32)

        def body(i, carry):
            for name in self.NAMES:
                for c in range(3):
                    getattr(self, name)[c, i] = zero
            for name in self.COEFF:
                getattr(self, name)[i] = zero
            return carry

        lax.fori_loop(0, self.shape[0], body, 0)

    def prepare(self, halo, gx0, gy0, xcount, ycount):
        w0, wn = self.window
        z = self.group
        s = self.scale
        lanes = lane(wn)
        first, last = lanes < z, lanes >= LANES - z
        rows = lax.broadcasted_iota(jnp.int32, (wn, LANES), 0) + (w0 - HY) + gy0
        inside_y = (rows >= 0) & (rows < ycount)
        w = slice(w0, w0 + wn)
        wm = slice(w0 - 1, w0 + wn - 1)
        wp = slice(w0 + 1, w0 + wn + 1)

        def body(i, carry):
            centre = self.k[i, w, :]
            behind = self.k[i, wm, :]
            ahead = self.k[i, wp, :]
            up, down = self.k[i + 1, w, :], self.k[i - 1, w, :]
            zp = jnp.where(last, 0.0, roll(centre, -z))
            zm = jnp.where(first, 0.0, roll(centre, z))
            total = 3.0 * centre + 0.5 * ((up + down) + (ahead + behind) + (zp + zm))
            diag = s * total + self.rea[i, w, :]
            self.dg[i, w, :] = diag
            self.kx[i, w, :] = (0.5 * s) * (centre + up)
            self.ky[i, wm, :] = (0.5 * s) * (behind + centre)
            self.kz[i, w, :] = jnp.where(last, 0.0, (0.5 * s) * (centre + zp))
            self.kzm[i, w, :] = jnp.where(first, 0.0, (0.5 * s) * (centre + zm))
            row = gx0 + i - HX
            inside = inside_y & (row >= 0) & (row < xcount)
            self.inv[i, w, :] = jnp.where(inside, 1.0 / (diag + 2.0 * BETA * s), 0.0)
            return carry

        lax.fori_loop(HX - halo, HX + self.xsize + halo, body, 0)

    def sweep(self, src, halo, window, consume):
        w0, wn = window
        z = self.group
        bs = BETA * self.scale
        lanes = lane(wn)
        first, last = lanes < z, lanes >= LANES - z
        w = slice(w0, w0 + wn)
        wm = slice(w0 - 1, w0 + wn - 1)
        wp = slice(w0 + 1, w0 + wn + 1)

        def div(i, rows, rows_next):
            uz = src[2, i, rows, :]
            total = src[0, i + 1, rows, :] - src[0, i, rows, :]
            total = total + (src[1, i, rows_next, :] - src[1, i, rows, :])
            return bs * (total + (jnp.where(last, 0.0, roll(uz, -z)) - uz))

        def body(i, before):
            here = div(i, w, wp)
            beside = div(i, wm, w)
            u = [src[c, i, w, :] for c in range(3)]
            under = jnp.where(first, bs * u[2], roll(here, z))
            gradients = (before, beside, under)
            kxp, kxm = self.kx[i, w, :], self.kx[i - 1, w, :]
            kyp, kym = self.ky[i, w, :], self.ky[i, wm, :]
            kzp, kzm = self.kz[i, w, :], self.kzm[i, w, :]
            dg = self.dg[i, w, :]
            out = []
            for c in range(3):
                near = kxp * src[c, i + 1, w, :] + kxm * src[c, i - 1, w, :]
                near = near + (kyp * src[c, i, wp, :] + kym * src[c, i, wm, :])
                near = near + (kzp * roll(u[c], -z) + kzm * roll(u[c], z))
                out.append(dg * u[c] - near + (gradients[c] - here))
            consume(i, w, u, out)
            return here

        lo = HX - halo
        lax.fori_loop(lo, HX + self.xsize + halo, body, div(lo - 1, w, wp))

    def step(self, src, dst, halo, number, window=None, out=None):
        rates = rate_list()

        def consume(i, w, u, au):
            inv = self.inv[i, w, :]
            for c in range(3):
                resid = self.f[c, i, w, :] - au[c]
                if number == 0:
                    p = (1.0 / THETA) * (inv * resid)
                else:
                    p = rates[number] * rates[number - 1] * self.p[c, i, w, :]
                    p = p + (2.0 * rates[number] / DELTA) * (inv * resid)
                if number < 3:
                    self.p[c, i, w, :] = p
                if out is not None:
                    out[c, i - HX] = u[c] + p
                else:
                    dst[c, i, w, :] = u[c] + p

        self.sweep(src, halo, window or self.window, consume)

    def first_direction(self, halo):
        w0, wn = self.window
        w = slice(w0, w0 + wn)

        def body(i, carry):
            inv = self.inv[i, w, :]
            for c in range(3):
                p = (1.0 / THETA) * (inv * self.f[c, i, w, :])
                self.p[c, i, w, :] = p
                self.xa[c, i, w, :] = p
            return carry

        lax.fori_loop(HX - halo, HX + self.xsize + halo, body, 0)

    def smooth_down(self, halo):
        self.step(self.xa, self.xb, max(halo - 1, 0), 1)
        self.step(self.xb, self.xa, max(halo - 2, 0), 2)
        self.step(self.xa, self.xb, max(halo - 3, 0), 3)

    def residual(self):
        def consume(i, w, u, au):
            for c in range(3):
                self.p[c, i, w, :] = self.f[c, i, w, :] - au[c]

        self.sweep(self.xb, 0, (HY, round8(self.ysize)), consume)

    def add_grown(self, coarse, xoff, yoff, temp):
        w0, wn = self.window
        w = slice(w0, w0 + wn)
        y0 = HY + (w0 - HY) // 2

        def body(j, carry):
            rows = pl.ds(yoff + y0, wn // 2)
            for c in range(3):
                value = coarse[c, j + (xoff + HX - 2), rows, :]
                temp[pl.ds(0, wn // 2, stride=2), :] = value
                temp[pl.ds(1, wn // 2, stride=2), :] = value
                grown = temp[0:wn, :]
                for t in range(2):
                    i = HX - 4 + 2 * j + t
                    self.xa[c, i, w, :] = self.xb[c, i, w, :] + grown
            return carry

        lax.fori_loop(0, (self.xsize + 8) // 2, body, 0)


def shrink_rows(load, xsize, ysize, group, store):
    def body(j, carry):
        total = None
        for x in range(2):
            for y in range(2):
                value = load(2 * j + x, y, ysize // 2)
                total = value if total is None else total + value
        store(j, 0.125 * halve_lanes(total, group))
        return carry

    lax.fori_loop(0, xsize // 2, body, 0)


def plan(xsize, ysize, groups, bricks):
    levels = []
    for number in range(3):
        size = ysize >> number
        levels.append(Level(number, xsize >> number, size, (HY - 4, round8(size + 8))))
    coarse = (xsize >> 3) * groups, (ysize >> 3) * bricks
    levels.append(Level(3, coarse[0], coarse[1], (HY, round8(coarse[1]))))
    size = xsize
    exchanges = dict(
        e0=Exchange(size, 1, 5, (4, 4, 4, 4, 5)),
        c1=Exchange(size // 2, 2, 3, (4, 5)),
        c2=Exchange(size // 4, 4, 1, (4, 4)),
        f1=Exchange(size // 2, 2, 2, (4, 4, 4)),
        f2=Exchange(size // 4, 4, 1, (4,) * 6),
        x0=Exchange(size, 1, 4, (4, 4, 4)),
        x1=Exchange(size // 2, 2, 2, (4, 4, 4)),
        x2=Exchange(size // 4, 4, 1, (4, 4, 4)),
        y2=Exchange(size // 4, 4, 1, (2, 2, 2)),
        y1=Exchange(size // 2, 2, 1, (2, 2, 2)),
    )
    return levels, exchanges


def cycle(groups, bricks, xsize, ysize, f_in, k_in, rea_in, out, *scratch):
    levels, exchanges = plan(xsize, ysize, groups, bricks)
    devices = groups * bricks
    g, b = lax.axis_index("grp"), lax.axis_index("brick")
    me = g * bricks + b
    exists = {}
    for dx, dy in DIRS:
        good = None
        for d, at, count in ((dx, g, groups), (dy, b, bricks)):
            if d:
                test = at > 0 if d < 0 else at < count - 1
                good = test if good is None else good & test
        exists[(dx, dy)] = good
    scratch = list(scratch)

    def take(count):
        got = scratch[:count]
        del scratch[:count]
        return got

    for level in levels:
        level.bind(take(12))
    for name in exchanges:
        exchanges[name].bind(take(6), (g, b, exists))
    temp, small, slot, slots, slot_send, slot_recv = take(6)
    ex = exchanges
    l0, l1, l2, l3 = levels

    barrier = pltpu.get_barrier_semaphore()

    def partner(n):
        other = (me + n) % devices
        return other // bricks, other % bricks

    def greet(n, carry):
        pl.semaphore_signal(
            barrier, inc=1, device_id=partner(n), device_id_type=pl.DeviceIdType.MESH
        )
        return carry

    lax.fori_loop(1, devices, greet, 0)

    def get_input(field, i, r0, count):
        rows = slice(r0, r0 + count)
        if field < 3:
            return f_in[field, i, rows, :]
        return (rea_in if field == 3 else k_in)[i, rows, :]

    ex["e0"].stage(get_input)
    pl.semaphore_wait(barrier, devices - 1)
    ex["e0"].start()

    for level in levels:
        level.clear()

    def load_own(i, carry):
        own = slice(HY, HY + ysize)
        for c in range(3):
            l0.f[c, HX + i, own, :] = f_in[c, i]
        l0.k[HX + i, own, :] = k_in[i]
        l0.rea[HX + i, own, :] = rea_in[i]
        return carry

    lax.fori_loop(0, xsize, load_own, 0)

    def shrink_field(fine, coarse, ref, target):
        def load(x, y, count):
            return ref[HX + x, pl.ds(HY + y, count, stride=2), :]

        def store(j, value):
            target[HX + j, HY : HY + value.shape[0], :] = value

        shrink_rows(load, fine.xsize, fine.ysize, fine.group, store)

    for fine, coarse in ((l0, l1), (l1, l2)):
        shrink_field(fine, coarse, fine.k, coarse.k)
        shrink_field(fine, coarse, fine.rea, coarse.rea)

    def getter(*refs):
        def get(field, i, r0, count):
            ref, c = refs[field]
            rows = slice(HY + r0, HY + r0 + count)
            return ref[HX + i, rows, :] if c is None else ref[c, HX + i, rows, :]

        return get

    def putter(*refs):
        def put(field, i, r0, value):
            ref, c = refs[field]
            rows = slice(HY + r0, HY + r0 + value.shape[0])
            if c is None:
                ref[HX + i, rows, :] = value
            else:
                ref[c, HX + i, rows, :] = value

        return put

    def three(ref):
        return tuple((ref, c) for c in range(3))

    def own_prepare(level, halo):
        xs, ys = level.xsize, level.ysize
        level.prepare(halo, g * xs, b * ys, xs * groups, ys * bricks)

    ex["c1"].stage(getter((l1.rea, None), (l1.k, None)))
    ex["c2"].stage(getter((l2.rea, None), (l2.k, None)))
    ex["e0"].finish(putter(*three(l0.f), (l0.rea, None), (l0.k, None)))
    ex["c1"].start()
    ex["c2"].start()

    def shrink_residual(fine, coarse):
        for c in range(3):
            shrink_field(fine, coarse, fine.p.at[c], coarse.f.at[c])

    own_prepare(l0, 4)
    l0.first_direction(4)
    l0.smooth_down(4)
    l0.residual()
    shrink_residual(l0, l1)

    ex["f1"].stage(getter(*three(l1.f)))
    ex["f1"].start()
    ex["x0"].stage(getter(*three(l0.xb)))
    ex["c1"].finish(putter((l1.rea, None), (l1.k, None)))
    ex["c2"].finish(putter((l2.rea, None), (l2.k, None)))
    own_prepare(l1, 4)
    own_prepare(l2, 4)
    ex["f1"].finish(putter(*three(l1.f)))
    ex["x0"].start()
    l1.first_direction(4)
    l1.smooth_down(4)
    l1.residual()
    shrink_residual(l1, l2)

    l2.first_direction(0)
    ex["f2"].stage(getter(*three(l2.f), *three(l2.p)))
    ex["f2"].start()
    ex["x1"].stage(getter(*three(l1.xb)))

    def put_f2(field, i, r0, value):
        putter(*three(l2.f), *three(l2.p))(field, i, r0, value)
        if field >= 3:
            putter(*three(l2.xa))(field - 3, i, r0, value)

    ex["f2"].finish(put_f2)
    ex["x1"].start()
    l2.smooth_down(4)
    ex["x2"].stage(getter(*three(l2.xb)))
    ex["x2"].start()
    l2.residual()

    def load_fine(field, x, y):
        rows = slice(HY + y, HY + y + 1)
        if field < 3:
            return l2.p[field, HX + x, rows, :]
        return (l2.rea if field == 3 else l2.k)[HX + x, rows, :]

    slot[...] = jnp.zeros_like(slot)
    for field in range(5):
        values = []
        for x in range(2):
            for y in range(2):
                total = load_fine(field, 2 * x, 2 * y) + load_fine(field, 2 * x, 2 * y + 1)
                total = total + load_fine(field, 2 * x + 1, 2 * y)
                total = total + load_fine(field, 2 * x + 1, 2 * y + 1)
                values.append(0.125 * halve_lanes(total, 4))
        slot[field : field + 1, :] = pack(values, 8)

    def gather_copy(n):
        return pltpu.make_async_remote_copy(
            src_ref=slot,
            dst_ref=slots.at[me],
            send_sem=slot_send.at[n],
            recv_sem=slot_recv.at[me],
            device_id=partner(n),
            device_id_type=pl.DeviceIdType.MESH,
        )

    def send_slot(n, carry):
        gather_copy(n).start()
        return carry

    lax.fori_loop(1, devices, send_slot, 0)

    def place(value, owner):
        og, ob = owner // bricks, owner % bricks
        for x in range(2):
            for y in range(2):
                small[...] = unpack(value, 8, 2 * x + y)
                row, col = HX + 2 * og + x, HY + 2 * ob + y
                for field in range(5):
                    line = small[field : field + 1, :]
                    if field < 3:
                        l3.f[field, row, pl.ds(col, 1), :] = line
                    else:
                        (l3.rea if field == 3 else l3.k)[row, pl.ds(col, 1), :] = line

    place(slot[...], me)

    def receive(n, carry):
        owner = (me + n) % devices
        pltpu.make_async_remote_copy(
            src_ref=slot,
            dst_ref=slots.at[owner],
            send_sem=slot_send.at[n],
            recv_sem=slot_recv.at[owner],
            device_id=partner(n),
            device_id_type=pl.DeviceIdType.MESH,
        ).wait_recv()
        place(slots[owner], owner)
        return carry

    lax.fori_loop(1, devices, receive, 0)
    l3.prepare(0, 0, 0, l3.xsize, l3.ysize)
    edge = slice(l3.window[0], l3.window[0] + l3.window[1])
    l3.kx[HX - 1, edge, :] = (0.5 * l3.scale) * l3.k[HX, edge, :]
    l3.first_direction(0)
    l3.smooth_down(0)

    ex["x2"].finish(putter(*three(l2.xb)))
    l2.add_grown(l3.xb, g * (xsize // 8), b * (ysize // 8), temp)
    up(l2)
    ex["y2"].stage(getter(*three(l2.xa)))
    ex["y2"].start()
    ex["x1"].finish(putter(*three(l1.xb)))
    ex["y2"].finish(putter(*three(l2.xa)))
    l1.add_grown(l2.xa, 0, 0, temp)
    up(l1)
    ex["y1"].stage(getter(*three(l1.xa)))
    ex["y1"].start()
    ex["x0"].finish(putter(*three(l0.xb)))
    ex["y1"].finish(putter(*three(l1.xa)))
    l0.add_grown(l1.xa, 0, 0, temp)
    up(l0, out)

    for name in ex:
        ex[name].finish_send()

    def sent(n, carry):
        gather_copy(n).wait_send()
        return carry

    lax.fori_loop(1, devices, sent, 0)


def up(level, out=None):
    level.step(level.xa, level.xb, 3, 0)
    level.step(level.xb, level.xa, 2, 1)
    level.step(level.xa, level.xb, 1, 2)
    level.step(level.xb, level.xa, 0, 3, (HY, round8(level.ysize)), out)


def on_device(right_side, stiffness, reaction):
    groups, bricks = lax.axis_size("grp"), lax.axis_size("brick")
    _, xsize, ysize, _ = right_side.shape
    levels, exchanges = plan(xsize, ysize, groups, bricks)
    devices = groups * bricks
    scratch = []
    for level in levels:
        scratch += level.scratch()
    for name in exchanges:
        scratch += exchanges[name].scratch()
    scratch += [
        pltpu.VMEM((32, LANES), jnp.float32),
        pltpu.VMEM((8, LANES), jnp.float32),
        pltpu.VMEM((8, LANES), jnp.float32),
        pltpu.VMEM((devices, 8, LANES), jnp.float32),
        pltpu.SemaphoreType.DMA((devices,)),
        pltpu.SemaphoreType.DMA((devices,)),
    ]

    def kernel(*refs):
        cycle(groups, bricks, xsize, ysize, *refs)

    vmem = pl.BlockSpec(memory_space=pltpu.VMEM)
    return pl.pallas_call(
        kernel,
        out_shape=jax.ShapeDtypeStruct(right_side.shape, jnp.float32),
        in_specs=[vmem] * 3,
        out_specs=vmem,
        scratch_shapes=scratch,
        compiler_params=pltpu.CompilerParams(
            collective_id=0, has_side_effects=True, vmem_limit_bytes=56 * 2**20
        ),
    )(right_side, stiffness, reaction)


def solution(mesh):
    in_specs = (P(None, "grp", "brick", None), P("grp", "brick", None), P("grp", "brick", None))
    out_specs = P(None, "grp", "brick", None)
    return jax.shard_map(
        on_device, mesh=mesh, in_specs=in_specs, out_specs=out_specs, check_vma=False
    )
```

```python
import jax
import jax.numpy as jnp
from jax import lax
from jax.experimental import pallas as pl
from jax.experimental.pallas import tpu as pltpu
from jax.sharding import PartitionSpec as P

BETA = 1.0
THETA = 1.5
DELTA = 1.0
SIGMA = 1.5
HX = 6
HY = 8
LANES = 128
DIRS = [(a, b) for a in (-1, 0, 1) for b in (-1, 0, 1) if (a, b) != (0, 0)]


def rate_list():
    rates = [1.0 / SIGMA]
    for number in range(3):
        rates.append(1.0 / (2.0 * SIGMA - rates[-1]))
    return rates


def round8(number):
    return -(-number // 8) * 8


def lane(rows):
    return lax.broadcasted_iota(jnp.int32, (rows, LANES), 1)


def roll(value, shift):
    return pltpu.roll(value, shift % LANES, 1)


def pack(values, group):
    if group == 1:
        return values[0]
    place = lane(values[0].shape[0]) % group
    out = values[0]
    for t in range(1, len(values)):
        out = jnp.where(place == t, values[t], out)
    return out


def unpack(value, group, t):
    if group == 1:
        return value
    out = jnp.where(lane(value.shape[0]) % group == t, value, 0.0)
    if t:
        out = roll(out, -t)
    shift = 1
    while shift < group:
        out = out + roll(out, shift)
        shift *= 2
    return out


def halve_lanes(value, group):
    first = lane(value.shape[0]) % (2 * group) < group
    return value + jnp.where(first, roll(value, -group), roll(value, group))


def rows_loop(start, count, most, body, carry=None):
    each = max(n for n in range(1, most + 1) if count % n == 0)
    if count == each:
        return body([start + t for t in range(each)], carry)

    def step(n, carry):
        out = body([start + n * each + t for t in range(each)], carry)
        return 0 if out is None else out

    return lax.fori_loop(0, count // each, step, 0 if carry is None else carry)


class Exchange:
    def __init__(self, size, group, packed, widths):
        self.size, self.group, self.packed, self.widths = size, group, packed, widths
        self.blocks = size // group
        self.offs = [sum(widths[:n]) for n in range(len(widths))]
        self.width = sum(widths)
        self.side_rows = round8(self.blocks * self.width)
        self.corner_rows = round8(packed * self.width)
        self.front_rows = round8(packed * len(widths) * size)

    def scratch(self):
        both = [
            pltpu.VMEM((2, self.front_rows, LANES), jnp.float32),
            pltpu.VMEM((2, self.side_rows, LANES), jnp.float32),
            pltpu.VMEM((4, self.corner_rows, LANES), jnp.float32),
        ]
        return both + both + [pltpu.SemaphoreType.DMA((8,)), pltpu.SemaphoreType.DMA((8,))]

    def bind(self, refs, where):
        self.sx, self.sy, self.sc, self.rx, self.ry, self.rc, self.ssem, self.rsem = refs
        self.where = where

    def copy(self, ex, ey):
        g, b, _ = self.where
        if ey == 0:
            side = 0 if ex < 0 else 1
            src, dst = self.sx.at[side], self.rx.at[1 - side]
        elif ex == 0:
            side = 0 if ey < 0 else 1
            src, dst = self.sy.at[side], self.ry.at[1 - side]
        else:
            side = (1 if ex > 0 else 0) * 2 + (1 if ey > 0 else 0)
            src, dst = self.sc.at[side], self.rc.at[3 - side]
        return pltpu.make_async_remote_copy(
            src_ref=src,
            dst_ref=dst,
            send_sem=self.ssem.at[DIRS.index((ex, ey))],
            recv_sem=self.rsem.at[DIRS.index((-ex, -ey))],
            device_id=(g + ex, b + ey),
            device_id_type=pl.DeviceIdType.MESH,
        )

    def stage(self, get):
        size, group, last = self.size, self.group, self.blocks - self.packed

        def load(field, j, r0, count):
            return pack([get(field, j * group + t, r0, count) for t in range(group)], group)

        for j in range(self.blocks):
            for field, width in enumerate(self.widths):
                for side in (0, 1):
                    value = load(field, j, 0 if side == 0 else size - width, width)
                    at = j * self.width + self.offs[field]
                    self.sy[side, at : at + width, :] = value
                    if j < self.packed:
                        self.sc[side, at : at + width, :] = value
                    if j >= last:
                        at = (j - last) * self.width + self.offs[field]
                        self.sc[2 + side, at : at + width, :] = value
        for side in (0, 1):
            for j in range(self.packed):
                for field in range(len(self.widths)):
                    at = (j * len(self.widths) + field) * size
                    value = load(field, j if side == 0 else last + j, 0, size)
                    self.sx[side, at : at + size, :] = value

    def start(self):
        exists = self.where[2]
        for d in DIRS:
            @pl.when(exists[d])
            def _(d=d):
                self.copy(*d).start()

    def finish_send(self):
        exists = self.where[2]
        for d in DIRS:
            @pl.when(exists[d])
            def _(d=d):
                self.copy(*d).wait_send()

    def finish(self, put):
        exists = self.where[2]
        size, group = self.size, self.group

        def spread_rows(value, x0, field, y0):
            for t in range(group):
                put(field, x0 + t, y0, unpack(value, group, t))

        for d in DIRS:
            @pl.when(exists[d])
            def _(d=d):
                dx, dy = d
                self.copy(-dx, -dy).wait_recv()
                xside, yside = (0 if dx < 0 else 1), (0 if dy < 0 else 1)
                base = {-1: -self.packed * group, 0: 0, 1: size}[dx]
                for j in range(self.packed if dx else self.blocks):
                    for field, width in enumerate(self.widths):
                        if dy == 0:
                            at = (j * len(self.widths) + field) * size
                            value, y0 = self.rx[xside, at : at + size, :], 0
                        else:
                            at = j * self.width + self.offs[field]
                            rows = slice(at, at + width)
                            if dx == 0:
                                value = self.ry[yside, rows, :]
                            else:
                                value = self.rc[2 * xside + yside, rows, :]
                            y0 = -width if dy < 0 else size
                        spread_rows(value, base + j * group, field, y0)


class Level:
    NAMES = ("f", "xa", "xb", "p")
    COEFF = ("k", "rea", "kx", "ky", "kz", "kzm", "dg", "inv")

    def __init__(self, number, xsize, ysize, window):
        self.number, self.xsize, self.ysize, self.window = number, xsize, ysize, window
        self.group = 2**number
        self.scale = 0.25**number
        self.shape = (xsize + 2 * HX, round8(ysize) + 2 * HY, LANES)

    def scratch(self):
        f32 = jnp.float32
        return [pltpu.VMEM((3,) + self.shape, f32) for _ in self.NAMES] + [
            pltpu.VMEM(self.shape, f32) for _ in self.COEFF
        ]

    def bind(self, refs):
        for name, ref in zip(self.NAMES + self.COEFF, refs):
            setattr(self, name, ref)

    def clear(self):
        zero = jnp.zeros(self.shape[1:], jnp.float32)

        def body(i, carry):
            for name in self.NAMES:
                for c in range(3):
                    getattr(self, name)[c, i] = zero
            for name in self.COEFF:
                getattr(self, name)[i] = zero
            return carry

        lax.fori_loop(0, self.shape[0], body, 0)

    def prepare(self, halo, gx0, gy0, xcount, ycount):
        w0, wn = self.window
        z = self.group
        s = self.scale
        lanes = lane(wn)
        first, last = lanes < z, lanes >= LANES - z
        rows = lax.broadcasted_iota(jnp.int32, (wn, LANES), 0) + (w0 - HY) + gy0
        inside_y = (rows >= 0) & (rows < ycount)
        w = slice(w0, w0 + wn)
        wm = slice(w0 - 1, w0 + wn - 1)
        wp = slice(w0 + 1, w0 + wn + 1)

        def one(i):
            centre = self.k[i, w, :]
            behind = self.k[i, wm, :]
            ahead = self.k[i, wp, :]
            up, down = self.k[i + 1, w, :], self.k[i - 1, w, :]
            zp = jnp.where(last, 0.0, roll(centre, -z))
            zm = jnp.where(first, 0.0, roll(centre, z))
            total = 3.0 * centre + 0.5 * ((up + down) + (ahead + behind) + (zp + zm))
            diag = s * total + self.rea[i, w, :]
            row = gx0 + i - HX
            inside = inside_y & (row >= 0) & (row < xcount)
            return (
                diag,
                (0.5 * s) * (centre + up),
                (0.5 * s) * (behind + centre),
                jnp.where(last, 0.0, (0.5 * s) * (centre + zp)),
                jnp.where(first, 0.0, (0.5 * s) * (centre + zm)),
                jnp.where(inside, 1.0 / (diag + 2.0 * BETA * s), 0.0),
            )

        def body(rows, carry):
            for i, values in [(i, one(i)) for i in rows]:
                self.dg[i, w, :] = values[0]
                self.kx[i, w, :] = values[1]
                self.ky[i, wm, :] = values[2]
                self.kz[i, w, :] = values[3]
                self.kzm[i, w, :] = values[4]
                self.inv[i, w, :] = values[5]

        rows_loop(HX - halo, self.xsize + 2 * halo, 4, body)

    def sweep(self, src, halo, window, consume):
        w0, wn = window
        z = self.group
        bs = BETA * self.scale
        lanes = lane(wn)
        first, last = lanes < z, lanes >= LANES - z
        w = slice(w0, w0 + wn)
        wm = slice(w0 - 1, w0 + wn - 1)
        wp = slice(w0 + 1, w0 + wn + 1)

        def flat(i, rows, rows_next):
            total = src[0, i + 1, rows, :] - src[0, i, rows, :]
            return total + (src[1, i, rows_next, :] - src[1, i, rows, :])

        def div(part, uz, ahead):
            return bs * (part + (jnp.where(last, 0.0, ahead) - uz))

        def one(i, before):
            u = [src[c, i, w, :] for c in range(3)]
            ahead = [roll(u[c], -z) for c in range(3)]
            behind = [roll(u[c], z) for c in range(3)]
            part = flat(i, w, wp)
            here = div(part, u[2], ahead[2])
            side_z = src[2, i, wm, :]
            beside = div(flat(i, wm, w), side_z, roll(side_z, -z))
            under = bs * (u[2] + jnp.where(first, 0.0, roll(part - u[2], z)))
            gradients = (before, beside, under)
            kxp, kxm = self.kx[i, w, :], self.kx[i - 1, w, :]
            kyp, kym = self.ky[i, w, :], self.ky[i, wm, :]
            kzp, kzm = self.kz[i, w, :], self.kzm[i, w, :]
            dg = self.dg[i, w, :]
            out = []
            for c in range(3):
                near = kxp * src[c, i + 1, w, :] + kxm * src[c, i - 1, w, :]
                near = near + (kyp * src[c, i, wp, :] + kym * src[c, i, wm, :])
                near = near + (kzp * ahead[c] + kzm * behind[c])
                out.append(dg * u[c] - near + (gradients[c] - here))
            return consume(i, w, u, out), here

        def body(rows, before):
            stores = []
            for i in rows:
                more, before = one(i, before)
                stores += more
            for ref, index, value in stores:
                ref[index] = value
            return before

        lo = HX - halo
        uz = src[2, lo - 1, w, :]
        before = div(flat(lo - 1, w, wp), uz, roll(uz, -z))
        most = 4 if self.number == 0 else 7
        rows_loop(lo, self.xsize + 2 * halo, most, body, before)

    def step(self, src, dst, halo, number, window=None, out=None):
        rates = rate_list()

        def consume(i, w, u, au):
            inv = self.inv[i, w, :]
            stores = []
            for c in range(3):
                resid = self.f[c, i, w, :] - au[c]
                if number == 0:
                    p = (1.0 / THETA) * (inv * resid)
                else:
                    p = rates[number] * rates[number - 1] * self.p[c, i, w, :]
                    p = p + (2.0 * rates[number] / DELTA) * (inv * resid)
                at = (c, i, w, slice(None))
                if number < 3:
                    stores.append((self.p, at, p))
                if out is not None:
                    stores.append((out, (c, i - HX), u[c] + p))
                else:
                    stores.append((dst, at, u[c] + p))
            return stores

        self.sweep(src, halo, window or self.window, consume)

    def first_direction(self, halo):
        w0, wn = self.window
        w = slice(w0, w0 + wn)

        def body(rows, carry):
            stores = []
            for i in rows:
                inv = (1.0 / THETA) * self.inv[i, w, :]
                stores += [(i, c, inv * self.f[c, i, w, :]) for c in range(3)]
            for i, c, p in stores:
                self.p[c, i, w, :] = p
                self.xa[c, i, w, :] = p

        rows_loop(HX - halo, self.xsize + 2 * halo, 4, body)

    def smooth_down(self, halo):
        self.step(self.xa, self.xb, max(halo - 1, 0), 1)
        self.step(self.xb, self.xa, max(halo - 2, 0), 2)
        self.step(self.xa, self.xb, max(halo - 3, 0), 3)

    def residual(self):
        def consume(i, w, u, au):
            at = [(c, i, w, slice(None)) for c in range(3)]
            return [(self.p, at[c], self.f[c, i, w, :] - au[c]) for c in range(3)]

        self.sweep(self.xb, 0, (HY, round8(self.ysize)), consume)

    def add_grown(self, coarse, xoff, yoff, temp):
        w0, wn = self.window
        w = slice(w0, w0 + wn)
        half = wn // 2
        rows = pl.ds(yoff + HY + (w0 - HY) // 2, half)

        def body(js, carry):
            for n, j in enumerate(js):
                for c in range(3):
                    value = coarse[c, j + (xoff + HX - 2), rows, :]
                    temp[3 * n + c, pl.ds(0, half, stride=2), :] = value
                    temp[3 * n + c, pl.ds(1, half, stride=2), :] = value
            for n, j in enumerate(js):
                for c in range(3):
                    grown = temp[3 * n + c, 0:wn, :]
                    for t in range(2):
                        i = HX - 4 + 2 * j + t
                        self.xa[c, i, w, :] = self.xb[c, i, w, :] + grown

        rows_loop(0, (self.xsize + 8) // 2, 4, body)


def shrink_fields(fine, pairs):
    half = fine.ysize // 2

    def body(js, carry):
        values = []
        for j in js:
            for load, store in pairs:
                total = load(2 * j, 0, half) + load(2 * j, 1, half)
                total = total + (load(2 * j + 1, 0, half) + load(2 * j + 1, 1, half))
                values.append((store, j, 0.125 * halve_lanes(total, fine.group)))
        for store, j, value in values:
            store(j, value)

    rows_loop(0, fine.xsize // 2, 4, body)


def plan(xsize, ysize, groups, bricks):
    levels = []
    for number in range(3):
        size = ysize >> number
        levels.append(Level(number, xsize >> number, size, (HY - 4, round8(size + 8))))
    coarse = (xsize >> 3) * groups, (ysize >> 3) * bricks
    levels.append(Level(3, coarse[0], coarse[1], (HY, round8(coarse[1]))))
    size = xsize
    exchanges = dict(
        c0=Exchange(size, 1, 5, (4, 5)),
        f0=Exchange(size, 1, 4, (4, 4, 4)),
        c1=Exchange(size // 2, 2, 3, (4, 5)),
        c2=Exchange(size // 4, 4, 1, (4, 4)),
        f1=Exchange(size // 2, 2, 2, (4, 4, 4)),
        f2=Exchange(size // 4, 4, 1, (4,) * 6),
        x0=Exchange(size, 1, 4, (4, 4, 4)),
        x1=Exchange(size // 2, 2, 2, (4, 4, 4)),
        x2=Exchange(size // 4, 4, 1, (4, 4, 4)),
        y2=Exchange(size // 4, 4, 1, (2, 2, 2)),
        y1=Exchange(size // 2, 2, 1, (2, 2, 2)),
    )
    return levels, exchanges


def cycle(groups, bricks, xsize, ysize, f_in, k_in, rea_in, out, *scratch):
    levels, exchanges = plan(xsize, ysize, groups, bricks)
    devices = groups * bricks
    g, b = lax.axis_index("grp"), lax.axis_index("brick")
    me = g * bricks + b
    exists = {}
    for dx, dy in DIRS:
        good = None
        for d, at, count in ((dx, g, groups), (dy, b, bricks)):
            if d:
                test = at > 0 if d < 0 else at < count - 1
                good = test if good is None else good & test
        exists[(dx, dy)] = good
    scratch = list(scratch)

    def take(count):
        got = scratch[:count]
        del scratch[:count]
        return got

    for level in levels:
        level.bind(take(12))
    for name in exchanges:
        exchanges[name].bind(take(8), (g, b, exists))
    temp, slot, slots, slot_send, slot_recv = take(5)
    ex = exchanges
    l0, l1, l2, l3 = levels

    barrier = pltpu.get_barrier_semaphore()

    def partner(n):
        other = (me + n) % devices
        return other // bricks, other % bricks

    def greet(n, carry):
        pl.semaphore_signal(
            barrier, inc=1, device_id=partner(n), device_id_type=pl.DeviceIdType.MESH
        )
        return carry

    lax.fori_loop(1, devices, greet, 0)

    def get_coeff(field, i, r0, count):
        return (rea_in, k_in)[field][i, r0 : r0 + count, :]

    def get_source(field, i, r0, count):
        return f_in[field, i, r0 : r0 + count, :]

    ex["c0"].stage(get_coeff)
    pl.semaphore_wait(barrier, devices - 1)
    ex["c0"].start()
    ex["f0"].stage(get_source)
    ex["f0"].start()

    for level in levels:
        level.clear()

    def load_own(i, carry):
        own = slice(HY, HY + ysize)
        for c in range(3):
            l0.f[c, HX + i, own, :] = f_in[c, i]
        l0.k[HX + i, own, :] = k_in[i]
        l0.rea[HX + i, own, :] = rea_in[i]
        return carry

    lax.fori_loop(0, xsize, load_own, 0)

    def shrink_pair(ref, target):
        def load(x, y, count):
            return ref[HX + x, pl.ds(HY + y, count, stride=2), :]

        def store(j, value):
            target[HX + j, HY : HY + value.shape[0], :] = value

        return load, store

    for fine, coarse in ((l0, l1), (l1, l2)):
        pairs = [shrink_pair(fine.k, coarse.k), shrink_pair(fine.rea, coarse.rea)]
        shrink_fields(fine, pairs)

    def getter(*refs):
        def get(field, i, r0, count):
            ref, c = refs[field]
            rows = slice(HY + r0, HY + r0 + count)
            return ref[HX + i, rows, :] if c is None else ref[c, HX + i, rows, :]

        return get

    def putter(*refs):
        def put(field, i, r0, value):
            ref, c = refs[field]
            rows = slice(HY + r0, HY + r0 + value.shape[0])
            if c is None:
                ref[HX + i, rows, :] = value
            else:
                ref[c, HX + i, rows, :] = value

        return put

    def three(ref):
        return tuple((ref, c) for c in range(3))

    def own_prepare(level, halo):
        xs, ys = level.xsize, level.ysize
        level.prepare(halo, g * xs, b * ys, xs * groups, ys * bricks)

    ex["c1"].stage(getter((l1.rea, None), (l1.k, None)))
    ex["c2"].stage(getter((l2.rea, None), (l2.k, None)))
    ex["c0"].finish(putter((l0.rea, None), (l0.k, None)))

    def shrink_residual(fine, coarse):
        pairs = [shrink_pair(fine.p.at[c], coarse.f.at[c]) for c in range(3)]
        shrink_fields(fine, pairs)

    own_prepare(l0, 4)
    ex["f0"].finish(putter(*three(l0.f)))
    ex["c1"].start()
    ex["c2"].start()
    l0.first_direction(4)
    l0.smooth_down(4)
    l0.residual()
    shrink_residual(l0, l1)

    ex["f1"].stage(getter(*three(l1.f)))
    ex["f1"].start()
    ex["x0"].stage(getter(*three(l0.xb)))
    ex["c1"].finish(putter((l1.rea, None), (l1.k, None)))
    ex["c2"].finish(putter((l2.rea, None), (l2.k, None)))
    own_prepare(l1, 4)
    own_prepare(l2, 4)
    ex["f1"].finish(putter(*three(l1.f)))
    ex["x0"].start()
    l1.first_direction(4)
    l1.smooth_down(4)
    l1.residual()
    shrink_residual(l1, l2)

    l2.first_direction(0)
    ex["f2"].stage(getter(*three(l2.f), *three(l2.p)))
    ex["f2"].start()
    ex["x1"].stage(getter(*three(l1.xb)))

    def put_f2(field, i, r0, value):
        putter(*three(l2.f), *three(l2.p))(field, i, r0, value)
        if field >= 3:
            putter(*three(l2.xa))(field - 3, i, r0, value)

    ex["f2"].finish(put_f2)
    ex["x1"].start()
    l2.smooth_down(4)
    ex["x2"].stage(getter(*three(l2.xb)))
    ex["x2"].start()
    l2.residual()

    def load_fine(field, x, y):
        rows = slice(HY + y, HY + y + 1)
        if field < 3:
            return l2.p[field, HX + x, rows, :]
        return (l2.rea if field == 3 else l2.k)[HX + x, rows, :]

    slot[...] = jnp.zeros_like(slot)
    for field in range(5):
        values = []
        for x in range(2):
            for y in range(2):
                total = load_fine(field, 2 * x, 2 * y) + load_fine(field, 2 * x, 2 * y + 1)
                total = total + load_fine(field, 2 * x + 1, 2 * y)
                total = total + load_fine(field, 2 * x + 1, 2 * y + 1)
                values.append(0.125 * halve_lanes(total, 4))
        slot[field : field + 1, :] = pack(values, 8)

    def gather_copy(n):
        return pltpu.make_async_remote_copy(
            src_ref=slot,
            dst_ref=slots.at[pl.ds(me * 8, 8)],
            send_sem=slot_send.at[n],
            recv_sem=slot_recv.at[me],
            device_id=partner(n),
            device_id_type=pl.DeviceIdType.MESH,
        )

    def send_slot(n, carry):
        gather_copy(n).start()
        return carry

    lax.fori_loop(1, devices, send_slot, 0)

    slots[pl.ds(pl.multiple_of(me * 8, 8), 8), :] = slot[...]

    def receive(n, carry):
        owner = (me + n) % devices
        pltpu.make_async_remote_copy(
            src_ref=slot,
            dst_ref=slots.at[pl.ds(owner * 8, 8)],
            send_sem=slot_send.at[n],
            recv_sem=slot_recv.at[owner],
            device_id=partner(n),
            device_id_type=pl.DeviceIdType.MESH,
        ).wait_recv()
        return carry

    lax.fori_loop(1, devices, receive, 0)
    for og in range(groups):
        for field in range(5):
            value = slots[pl.ds(og * bricks * 8 + field, bricks, stride=8), :]
            for x in range(2):
                for y in range(2):
                    line = unpack(value, 8, 2 * x + y)
                    row, cols = HX + 2 * og + x, pl.ds(HY + y, bricks, stride=2)
                    if field < 3:
                        l3.f[field, row, cols, :] = line
                    else:
                        (l3.rea if field == 3 else l3.k)[row, cols, :] = line
    l3.prepare(0, 0, 0, l3.xsize, l3.ysize)
    edge = slice(l3.window[0], l3.window[0] + l3.window[1])
    l3.kx[HX - 1, edge, :] = (0.5 * l3.scale) * l3.k[HX, edge, :]
    l3.first_direction(0)
    l3.smooth_down(0)

    ex["x2"].finish(putter(*three(l2.xb)))
    l2.add_grown(l3.xb, g * (xsize // 8), b * (ysize // 8), temp)
    up(l2)
    ex["y2"].stage(getter(*three(l2.xa)))
    ex["y2"].start()
    ex["x1"].finish(putter(*three(l1.xb)))
    ex["y2"].finish(putter(*three(l2.xa)))
    l1.add_grown(l2.xa, 0, 0, temp)
    up(l1)
    ex["y1"].stage(getter(*three(l1.xa)))
    ex["y1"].start()
    ex["x0"].finish(putter(*three(l0.xb)))
    ex["y1"].finish(putter(*three(l1.xa)))
    l0.add_grown(l1.xa, 0, 0, temp)
    up(l0, out)

    for name in ex:
        ex[name].finish_send()

    def sent(n, carry):
        gather_copy(n).wait_send()
        return carry

    lax.fori_loop(1, devices, sent, 0)


def up(level, out=None):
    level.step(level.xa, level.xb, 3, 0)
    level.step(level.xb, level.xa, 2, 1)
    level.step(level.xa, level.xb, 1, 2)
    level.step(level.xb, level.xa, 0, 3, (HY, round8(level.ysize)), out)


def on_device(right_side, stiffness, reaction):
    groups, bricks = lax.axis_size("grp"), lax.axis_size("brick")
    _, xsize, ysize, _ = right_side.shape
    levels, exchanges = plan(xsize, ysize, groups, bricks)
    devices = groups * bricks
    scratch = []
    for level in levels:
        scratch += level.scratch()
    for name in exchanges:
        scratch += exchanges[name].scratch()
    scratch += [
        pltpu.VMEM((12, 32, LANES), jnp.float32),
        pltpu.VMEM((8, LANES), jnp.float32),
        pltpu.VMEM((8 * devices, LANES), jnp.float32),
        pltpu.SemaphoreType.DMA((devices,)),
        pltpu.SemaphoreType.DMA((devices,)),
    ]

    def kernel(*refs):
        cycle(groups, bricks, xsize, ysize, *refs)

    vmem = pl.BlockSpec(memory_space=pltpu.VMEM)
    return pl.pallas_call(
        kernel,
        out_shape=jax.ShapeDtypeStruct(right_side.shape, jnp.float32),
        in_specs=[vmem] * 3,
        out_specs=vmem,
        scratch_shapes=scratch,
        compiler_params=pltpu.CompilerParams(
            collective_id=0, has_side_effects=True, vmem_limit_bytes=56 * 2**20
        ),
    )(right_side, stiffness, reaction)


def solution(mesh):
    in_specs = (P(None, "grp", "brick", None), P("grp", "brick", None), P("grp", "brick", None))
    out_specs = P(None, "grp", "brick", None)
    return jax.shard_map(
        on_device, mesh=mesh, in_specs=in_specs, out_specs=out_specs, check_vma=False
    )
```

```python
import jax
import jax.numpy as jnp
from jax import lax
from jax.experimental import pallas as pl
from jax.experimental.pallas import tpu as pltpu
from jax.sharding import PartitionSpec as P

BETA = 1.0
THETA = 1.5
DELTA = 1.0
SIGMA = 1.5
HX = 6
HY = 8
LANES = 128
DIRS = [(a, b) for a in (-1, 0, 1) for b in (-1, 0, 1) if (a, b) != (0, 0)]


def rate_list():
    rates = [1.0 / SIGMA]
    for number in range(3):
        rates.append(1.0 / (2.0 * SIGMA - rates[-1]))
    return rates


def round8(number):
    return -(-number // 8) * 8


def lane(rows):
    return lax.broadcasted_iota(jnp.int32, (rows, LANES), 1)


def roll(value, shift):
    return pltpu.roll(value, shift % LANES, 1)


def pack(values, group):
    if group == 1:
        return values[0]
    place = lane(values[0].shape[0]) % group
    out = values[0]
    for t in range(1, len(values)):
        out = jnp.where(place == t, values[t], out)
    return out


def unpack(value, group, t):
    if group == 1:
        return value
    out = jnp.where(lane(value.shape[0]) % group == t, value, 0.0)
    if t:
        out = roll(out, -t)
    shift = 1
    while shift < group:
        out = out + roll(out, shift)
        shift *= 2
    return out


def halve_lanes(value, group):
    first = lane(value.shape[0]) % (2 * group) < group
    return value + jnp.where(first, roll(value, -group), roll(value, group))


def rows_loop(start, count, most, body, carry=None):
    each = max(n for n in range(1, most + 1) if count % n == 0)
    if count == each:
        return body([start + t for t in range(each)], carry)

    def step(n, carry):
        out = body([start + n * each + t for t in range(each)], carry)
        return 0 if out is None else out

    return lax.fori_loop(0, count // each, step, 0 if carry is None else carry)


class Exchange:
    def __init__(self, size, group, packed, widths):
        self.size, self.group, self.packed, self.widths = size, group, packed, widths
        self.blocks = size // group
        self.offs = [sum(widths[:n]) for n in range(len(widths))]
        self.width = sum(widths)
        self.side_rows = round8(self.blocks * self.width)
        self.corner_rows = round8(packed * self.width)
        self.front_rows = round8(packed * len(widths) * size)

    def scratch(self):
        both = [
            pltpu.VMEM((2, self.front_rows, LANES), jnp.float32),
            pltpu.VMEM((2, self.side_rows, LANES), jnp.float32),
            pltpu.VMEM((4, self.corner_rows, LANES), jnp.float32),
        ]
        return both + both + [pltpu.SemaphoreType.DMA((8,)), pltpu.SemaphoreType.DMA((8,))]

    def bind(self, refs, where):
        self.sx, self.sy, self.sc, self.rx, self.ry, self.rc, self.ssem, self.rsem = refs
        self.where = where

    def copy(self, ex, ey):
        g, b, _ = self.where
        if ey == 0:
            side = 0 if ex < 0 else 1
            src, dst = self.sx.at[side], self.rx.at[1 - side]
        elif ex == 0:
            side = 0 if ey < 0 else 1
            src, dst = self.sy.at[side], self.ry.at[1 - side]
        else:
            side = (1 if ex > 0 else 0) * 2 + (1 if ey > 0 else 0)
            src, dst = self.sc.at[side], self.rc.at[3 - side]
        return pltpu.make_async_remote_copy(
            src_ref=src,
            dst_ref=dst,
            send_sem=self.ssem.at[DIRS.index((ex, ey))],
            recv_sem=self.rsem.at[DIRS.index((-ex, -ey))],
            device_id=(g + ex, b + ey),
            device_id_type=pl.DeviceIdType.MESH,
        )

    def stage(self, get):
        size, group, last = self.size, self.group, self.blocks - self.packed

        def load(field, j, r0, count):
            return pack([get(field, j * group + t, r0, count) for t in range(group)], group)

        for j in range(self.blocks):
            for field, width in enumerate(self.widths):
                for side in (0, 1):
                    value = load(field, j, 0 if side == 0 else size - width, width)
                    at = j * self.width + self.offs[field]
                    self.sy[side, at : at + width, :] = value
                    if j < self.packed:
                        self.sc[side, at : at + width, :] = value
                    if j >= last:
                        at = (j - last) * self.width + self.offs[field]
                        self.sc[2 + side, at : at + width, :] = value
        for side in (0, 1):
            for j in range(self.packed):
                for field in range(len(self.widths)):
                    at = (j * len(self.widths) + field) * size
                    value = load(field, j if side == 0 else last + j, 0, size)
                    self.sx[side, at : at + size, :] = value

    def start(self):
        exists = self.where[2]
        for d in DIRS:
            @pl.when(exists[d])
            def _(d=d):
                self.copy(*d).start()

    def finish_send(self):
        exists = self.where[2]
        for d in DIRS:
            @pl.when(exists[d])
            def _(d=d):
                self.copy(*d).wait_send()

    def clear_absent(self):
        exists = self.where[2]
        for d in DIRS:
            @pl.when(jnp.logical_not(exists[d]))
            def _(d=d):
                ref = self.landing(*d)
                ref[...] = jnp.zeros(ref.shape, jnp.float32)

    def landing(self, dx, dy):
        xside, yside = (0 if dx < 0 else 1), (0 if dy < 0 else 1)
        if dy == 0:
            return self.rx.at[xside]
        return self.ry.at[yside] if dx == 0 else self.rc.at[2 * xside + yside]

    def finish(self, put):
        exists = self.where[2]
        size, group = self.size, self.group
        for dx, dy in DIRS:
            @pl.when(exists[(dx, dy)])
            def _(dx=dx, dy=dy):
                self.copy(-dx, -dy).wait_recv()

        for dx, dy in DIRS:
            ref = self.landing(dx, dy)
            base = {-1: -self.packed * group, 0: 0, 1: size}[dx]
            for j in range(self.packed if dx else self.blocks):
                for field, width in enumerate(self.widths):
                    if dy == 0:
                        at, count, y0 = (j * len(self.widths) + field) * size, size, 0
                    else:
                        at, count = j * self.width + self.offs[field], width
                        y0 = -width if dy < 0 else size
                    value = ref[at : at + count, :]
                    for t in range(group):
                        put(field, base + j * group + t, y0, unpack(value, group, t))


class Level:
    NAMES = ("f", "xa", "xb", "p")
    COEFF = ("k", "rea", "kx", "ky", "kz", "kzm", "dg", "inv")

    def __init__(self, number, xsize, ysize, window):
        self.number, self.xsize, self.ysize, self.window = number, xsize, ysize, window
        self.group = 2**number
        self.scale = 0.25**number
        self.shape = (xsize + 2 * HX, round8(ysize) + 2 * HY, LANES)

    def scratch(self):
        f32 = jnp.float32
        return [pltpu.VMEM((3,) + self.shape, f32) for _ in self.NAMES] + [
            pltpu.VMEM(self.shape, f32) for _ in self.COEFF
        ]

    def bind(self, refs):
        for name, ref in zip(self.NAMES + self.COEFF, refs):
            setattr(self, name, ref)

    def clear(self):
        zero = jnp.zeros(self.shape[1:], jnp.float32)

        def body(i, carry):
            for name in self.NAMES:
                for c in range(3):
                    getattr(self, name)[c, i] = zero
            for name in self.COEFF:
                getattr(self, name)[i] = zero
            return carry

        lax.fori_loop(0, self.shape[0], body, 0)

    def prepare(self, halo, gx0, gy0, xcount, ycount):
        w0, wn = self.window
        z = self.group
        s = self.scale
        lanes = lane(wn)
        first, last = lanes < z, lanes >= LANES - z
        rows = lax.broadcasted_iota(jnp.int32, (wn, LANES), 0) + (w0 - HY) + gy0
        inside_y = (rows >= 0) & (rows < ycount)
        w = slice(w0, w0 + wn)
        wm = slice(w0 - 1, w0 + wn - 1)
        wp = slice(w0 + 1, w0 + wn + 1)

        def one(i):
            centre = self.k[i, w, :]
            behind = self.k[i, wm, :]
            ahead = self.k[i, wp, :]
            up, down = self.k[i + 1, w, :], self.k[i - 1, w, :]
            zp = jnp.where(last, 0.0, roll(centre, -z))
            zm = jnp.where(first, 0.0, roll(centre, z))
            total = 3.0 * centre + 0.5 * ((up + down) + (ahead + behind) + (zp + zm))
            diag = s * total + self.rea[i, w, :]
            row = gx0 + i - HX
            inside = inside_y & (row >= 0) & (row < xcount)
            return (
                diag,
                (0.5 * s) * (centre + up),
                (0.5 * s) * (behind + centre),
                jnp.where(last, 0.0, (0.5 * s) * (centre + zp)),
                jnp.where(first, 0.0, (0.5 * s) * (centre + zm)),
                jnp.where(inside, 1.0 / (diag + 2.0 * BETA * s), 0.0),
            )

        def body(rows, carry):
            for i, values in [(i, one(i)) for i in rows]:
                self.dg[i, w, :] = values[0]
                self.kx[i, w, :] = values[1]
                self.ky[i, wm, :] = values[2]
                self.kz[i, w, :] = values[3]
                self.kzm[i, w, :] = values[4]
                self.inv[i, w, :] = values[5]

        rows_loop(HX - halo, self.xsize + 2 * halo, 4, body)

    def sweep(self, src, halo, window, consume):
        w0, wn = window
        z = self.group
        bs = BETA * self.scale
        lanes = lane(wn)
        first, last = lanes < z, lanes >= LANES - z
        w = slice(w0, w0 + wn)
        wm = slice(w0 - 1, w0 + wn - 1)
        wp = slice(w0 + 1, w0 + wn + 1)

        def flat(i, rows, rows_next):
            total = src[0, i + 1, rows, :] - src[0, i, rows, :]
            return total + (src[1, i, rows_next, :] - src[1, i, rows, :])

        def div(part, uz, ahead):
            return bs * (part + (jnp.where(last, 0.0, ahead) - uz))

        def one(i, before):
            u = [src[c, i, w, :] for c in range(3)]
            ahead = [roll(u[c], -z) for c in range(3)]
            behind = [roll(u[c], z) for c in range(3)]
            part = flat(i, w, wp)
            here = div(part, u[2], ahead[2])
            side_z = src[2, i, wm, :]
            beside = div(flat(i, wm, w), side_z, roll(side_z, -z))
            under = bs * (u[2] + jnp.where(first, 0.0, roll(part - u[2], z)))
            gradients = (before, beside, under)
            kxp, kxm = self.kx[i, w, :], self.kx[i - 1, w, :]
            kyp, kym = self.ky[i, w, :], self.ky[i, wm, :]
            kzp, kzm = self.kz[i, w, :], self.kzm[i, w, :]
            dg = self.dg[i, w, :]
            out = []
            for c in range(3):
                near = kxp * src[c, i + 1, w, :] + kxm * src[c, i - 1, w, :]
                near = near + (kyp * src[c, i, wp, :] + kym * src[c, i, wm, :])
                near = near + (kzp * ahead[c] + kzm * behind[c])
                out.append(dg * u[c] - near + (gradients[c] - here))
            return consume(i, w, u, out), here

        def body(rows, before):
            stores = []
            for i in rows:
                more, before = one(i, before)
                stores += more
            for ref, index, value in stores:
                ref[index] = value
            return before

        lo = HX - halo
        uz = src[2, lo - 1, w, :]
        before = div(flat(lo - 1, w, wp), uz, roll(uz, -z))
        most = 4 if self.number == 0 else 7
        rows_loop(lo, self.xsize + 2 * halo, most, body, before)

    def step(self, src, dst, halo, number, window=None, out=None):
        rates = rate_list()

        def consume(i, w, u, au):
            inv = self.inv[i, w, :]
            stores = []
            for c in range(3):
                resid = self.f[c, i, w, :] - au[c]
                if number == 0:
                    p = (1.0 / THETA) * (inv * resid)
                else:
                    p = rates[number] * rates[number - 1] * self.p[c, i, w, :]
                    p = p + (2.0 * rates[number] / DELTA) * (inv * resid)
                at = (c, i, w, slice(None))
                if number < 3:
                    stores.append((self.p, at, p))
                if out is not None:
                    stores.append((out, (c, i - HX), u[c] + p))
                else:
                    stores.append((dst, at, u[c] + p))
            return stores

        self.sweep(src, halo, window or self.window, consume)

    def first_direction(self, halo):
        w0, wn = self.window
        w = slice(w0, w0 + wn)

        def body(rows, carry):
            stores = []
            for i in rows:
                inv = (1.0 / THETA) * self.inv[i, w, :]
                stores += [(i, c, inv * self.f[c, i, w, :]) for c in range(3)]
            for i, c, p in stores:
                self.p[c, i, w, :] = p
                self.xa[c, i, w, :] = p

        rows_loop(HX - halo, self.xsize + 2 * halo, 4, body)

    def smooth_down(self, halo):
        self.step(self.xa, self.xb, max(halo - 1, 0), 1)
        self.step(self.xb, self.xa, max(halo - 2, 0), 2)
        self.step(self.xa, self.xb, max(halo - 3, 0), 3)

    def residual(self):
        def consume(i, w, u, au):
            at = [(c, i, w, slice(None)) for c in range(3)]
            return [(self.p, at[c], self.f[c, i, w, :] - au[c]) for c in range(3)]

        self.sweep(self.xb, 0, (HY, round8(self.ysize)), consume)

    def add_grown(self, coarse, xoff, yoff, temp):
        w0, wn = self.window
        w = slice(w0, w0 + wn)
        half = wn // 2
        rows = pl.ds(yoff + HY + (w0 - HY) // 2, half)

        def body(js, carry):
            for n, j in enumerate(js):
                for c in range(3):
                    value = coarse[c, j + (xoff + HX - 2), rows, :]
                    temp[3 * n + c, pl.ds(0, half, stride=2), :] = value
                    temp[3 * n + c, pl.ds(1, half, stride=2), :] = value
            for n, j in enumerate(js):
                for c in range(3):
                    grown = temp[3 * n + c, 0:wn, :]
                    for t in range(2):
                        i = HX - 4 + 2 * j + t
                        self.xa[c, i, w, :] = self.xb[c, i, w, :] + grown

        rows_loop(0, (self.xsize + 8) // 2, 4, body)


def shrink_fields(fine, pairs):
    half = fine.ysize // 2

    def body(js, carry):
        values = []
        for j in js:
            for load, store in pairs:
                total = load(2 * j, 0, half) + load(2 * j, 1, half)
                total = total + (load(2 * j + 1, 0, half) + load(2 * j + 1, 1, half))
                values.append((store, j, 0.125 * halve_lanes(total, fine.group)))
        for store, j, value in values:
            store(j, value)

    rows_loop(0, fine.xsize // 2, 4, body)


def plan(xsize, ysize, groups, bricks):
    levels = []
    for number in range(3):
        size = ysize >> number
        levels.append(Level(number, xsize >> number, size, (HY - 4, round8(size + 8))))
    coarse = (xsize >> 3) * groups, (ysize >> 3) * bricks
    levels.append(Level(3, coarse[0], coarse[1], (HY, round8(coarse[1]))))
    size = xsize
    exchanges = dict(
        c0=Exchange(size, 1, 5, (4, 5)),
        f0=Exchange(size, 1, 4, (4, 4, 4)),
        c1=Exchange(size // 2, 2, 3, (4, 5)),
        c2=Exchange(size // 4, 4, 1, (4, 4)),
        f1=Exchange(size // 2, 2, 2, (4, 4, 4)),
        f2=Exchange(size // 4, 4, 1, (4,) * 6),
        x0=Exchange(size, 1, 4, (4, 4, 4)),
        x1=Exchange(size // 2, 2, 2, (4, 4, 4)),
        x2=Exchange(size // 4, 4, 1, (4, 4, 4)),
        y2=Exchange(size // 4, 4, 1, (2, 2, 2)),
        y1=Exchange(size // 2, 2, 1, (2, 2, 2)),
    )
    return levels, exchanges


def cycle(groups, bricks, xsize, ysize, f_in, k_in, rea_in, out, *scratch):
    levels, exchanges = plan(xsize, ysize, groups, bricks)
    devices = groups * bricks
    g, b = lax.axis_index("grp"), lax.axis_index("brick")
    me = g * bricks + b
    exists = {}
    for dx, dy in DIRS:
        good = None
        for d, at, count in ((dx, g, groups), (dy, b, bricks)):
            if d:
                test = at > 0 if d < 0 else at < count - 1
                good = test if good is None else good & test
        exists[(dx, dy)] = good
    scratch = list(scratch)

    def take(count):
        got = scratch[:count]
        del scratch[:count]
        return got

    for level in levels:
        level.bind(take(12))
    for name in exchanges:
        exchanges[name].bind(take(8), (g, b, exists))
    temp, slot, slots, slot_send, slot_recv = take(5)
    ex = exchanges
    l0, l1, l2, l3 = levels

    barrier = pltpu.get_barrier_semaphore()

    def partner(n):
        other = (me + n) % devices
        return other // bricks, other % bricks

    def greet(n, carry):
        pl.semaphore_signal(
            barrier, inc=1, device_id=partner(n), device_id_type=pl.DeviceIdType.MESH
        )
        return carry

    lax.fori_loop(1, devices, greet, 0)

    def get_coeff(field, i, r0, count):
        return (rea_in, k_in)[field][i, r0 : r0 + count, :]

    def get_source(field, i, r0, count):
        return f_in[field, i, r0 : r0 + count, :]

    ex["c0"].stage(get_coeff)
    pl.semaphore_wait(barrier, devices - 1)
    ex["c0"].start()
    ex["f0"].stage(get_source)
    ex["f0"].start()

    for name in ex:
        ex[name].clear_absent()
    for level in levels:
        level.clear()

    def load_own(i, carry):
        own = slice(HY, HY + ysize)
        for c in range(3):
            l0.f[c, HX + i, own, :] = f_in[c, i]
        l0.k[HX + i, own, :] = k_in[i]
        l0.rea[HX + i, own, :] = rea_in[i]
        return carry

    lax.fori_loop(0, xsize, load_own, 0)

    def shrink_pair(ref, target):
        def load(x, y, count):
            return ref[HX + x, pl.ds(HY + y, count, stride=2), :]

        def store(j, value):
            target[HX + j, HY : HY + value.shape[0], :] = value

        return load, store

    for fine, coarse in ((l0, l1), (l1, l2)):
        pairs = [shrink_pair(fine.k, coarse.k), shrink_pair(fine.rea, coarse.rea)]
        shrink_fields(fine, pairs)

    def getter(*refs):
        def get(field, i, r0, count):
            ref, c = refs[field]
            rows = slice(HY + r0, HY + r0 + count)
            return ref[HX + i, rows, :] if c is None else ref[c, HX + i, rows, :]

        return get

    def putter(*refs):
        def put(field, i, r0, value):
            ref, c = refs[field]
            rows = slice(HY + r0, HY + r0 + value.shape[0])
            if c is None:
                ref[HX + i, rows, :] = value
            else:
                ref[c, HX + i, rows, :] = value

        return put

    def three(ref):
        return tuple((ref, c) for c in range(3))

    def own_prepare(level, halo):
        xs, ys = level.xsize, level.ysize
        level.prepare(halo, g * xs, b * ys, xs * groups, ys * bricks)

    ex["c1"].stage(getter((l1.rea, None), (l1.k, None)))
    ex["c2"].stage(getter((l2.rea, None), (l2.k, None)))
    ex["c0"].finish(putter((l0.rea, None), (l0.k, None)))

    def shrink_residual(fine, coarse):
        pairs = [shrink_pair(fine.p.at[c], coarse.f.at[c]) for c in range(3)]
        shrink_fields(fine, pairs)

    own_prepare(l0, 4)
    ex["f0"].finish(putter(*three(l0.f)))
    ex["c1"].start()
    ex["c2"].start()
    l0.first_direction(4)
    l0.smooth_down(4)
    l0.residual()
    shrink_residual(l0, l1)

    ex["f1"].stage(getter(*three(l1.f)))
    ex["f1"].start()
    ex["x0"].stage(getter(*three(l0.xb)))
    ex["c1"].finish(putter((l1.rea, None), (l1.k, None)))
    ex["c2"].finish(putter((l2.rea, None), (l2.k, None)))
    own_prepare(l1, 4)
    own_prepare(l2, 4)
    ex["f1"].finish(putter(*three(l1.f)))
    ex["x0"].start()
    l1.first_direction(4)
    l1.smooth_down(4)
    l1.residual()
    shrink_residual(l1, l2)

    l2.first_direction(0)
    ex["f2"].stage(getter(*three(l2.f), *three(l2.p)))
    ex["f2"].start()
    ex["x1"].stage(getter(*three(l1.xb)))

    def put_f2(field, i, r0, value):
        putter(*three(l2.f), *three(l2.p))(field, i, r0, value)
        if field >= 3:
            putter(*three(l2.xa))(field - 3, i, r0, value)

    for name in ("c0", "f0", "c1", "c2", "f1"):
        ex[name].finish_send()
    ex["f2"].finish(put_f2)
    ex["x1"].start()
    l2.smooth_down(4)
    ex["x2"].stage(getter(*three(l2.xb)))
    ex["x2"].start()
    l2.residual()

    def load_fine(field, x, y):
        rows = slice(HY + y, HY + y + 1)
        if field < 3:
            return l2.p[field, HX + x, rows, :]
        return (l2.rea if field == 3 else l2.k)[HX + x, rows, :]

    slot[...] = jnp.zeros_like(slot)
    for field in range(5):
        values = []
        for x in range(2):
            for y in range(2):
                total = load_fine(field, 2 * x, 2 * y) + load_fine(field, 2 * x, 2 * y + 1)
                total = total + load_fine(field, 2 * x + 1, 2 * y)
                total = total + load_fine(field, 2 * x + 1, 2 * y + 1)
                values.append(0.125 * halve_lanes(total, 4))
        slot[field : field + 1, :] = pack(values, 8)

    def gather_copy(n):
        return pltpu.make_async_remote_copy(
            src_ref=slot,
            dst_ref=slots.at[pl.ds(me * 8, 8)],
            send_sem=slot_send.at[n],
            recv_sem=slot_recv.at[me],
            device_id=partner(n),
            device_id_type=pl.DeviceIdType.MESH,
        )

    def send_slot(n, carry):
        gather_copy(n).start()
        return carry

    lax.fori_loop(1, devices, send_slot, 0)

    slots[pl.ds(pl.multiple_of(me * 8, 8), 8), :] = slot[...]

    def receive(n, carry):
        owner = (me + n) % devices
        pltpu.make_async_remote_copy(
            src_ref=slot,
            dst_ref=slots.at[pl.ds(owner * 8, 8)],
            send_sem=slot_send.at[n],
            recv_sem=slot_recv.at[owner],
            device_id=partner(n),
            device_id_type=pl.DeviceIdType.MESH,
        ).wait_recv()
        return carry

    lax.fori_loop(1, devices, receive, 0)
    for og in range(groups):
        for field in range(5):
            value = slots[pl.ds(og * bricks * 8 + field, bricks, stride=8), :]
            for x in range(2):
                for y in range(2):
                    line = unpack(value, 8, 2 * x + y)
                    row, cols = HX + 2 * og + x, pl.ds(HY + y, bricks, stride=2)
                    if field < 3:
                        l3.f[field, row, cols, :] = line
                    else:
                        (l3.rea if field == 3 else l3.k)[row, cols, :] = line
    l3.prepare(0, 0, 0, l3.xsize, l3.ysize)
    edge = slice(l3.window[0], l3.window[0] + l3.window[1])
    l3.kx[HX - 1, edge, :] = (0.5 * l3.scale) * l3.k[HX, edge, :]
    l3.first_direction(0)
    l3.smooth_down(0)

    ex["x2"].finish(putter(*three(l2.xb)))
    l2.add_grown(l3.xb, g * (xsize // 8), b * (ysize // 8), temp)
    up(l2)
    ex["y2"].stage(getter(*three(l2.xa)))
    ex["y2"].start()
    ex["x1"].finish(putter(*three(l1.xb)))

    def sent(n, carry):
        gather_copy(n).wait_send()
        return carry

    lax.fori_loop(1, devices, sent, 0)
    for name in ("f2", "x1", "x2"):
        ex[name].finish_send()
    ex["y2"].finish(putter(*three(l2.xa)))
    l1.add_grown(l2.xa, 0, 0, temp)
    up(l1)
    ex["y1"].stage(getter(*three(l1.xa)))
    ex["y1"].start()
    ex["x0"].finish(putter(*three(l0.xb)))
    ex["x0"].finish_send()
    ex["y2"].finish_send()
    ex["y1"].finish(putter(*three(l1.xa)))
    l0.add_grown(l1.xa, 0, 0, temp)
    up(l0, out)

    ex["y1"].finish_send()


def up(level, out=None):
    level.step(level.xa, level.xb, 3, 0)
    level.step(level.xb, level.xa, 2, 1)
    level.step(level.xa, level.xb, 1, 2)
    level.step(level.xb, level.xa, 0, 3, (HY, round8(level.ysize)), out)


def on_device(right_side, stiffness, reaction):
    groups, bricks = lax.axis_size("grp"), lax.axis_size("brick")
    _, xsize, ysize, _ = right_side.shape
    levels, exchanges = plan(xsize, ysize, groups, bricks)
    devices = groups * bricks
    scratch = []
    for level in levels:
        scratch += level.scratch()
    for name in exchanges:
        scratch += exchanges[name].scratch()
    scratch += [
        pltpu.VMEM((12, 32, LANES), jnp.float32),
        pltpu.VMEM((8, LANES), jnp.float32),
        pltpu.VMEM((8 * devices, LANES), jnp.float32),
        pltpu.SemaphoreType.DMA((devices,)),
        pltpu.SemaphoreType.DMA((devices,)),
    ]

    def kernel(*refs):
        cycle(groups, bricks, xsize, ysize, *refs)

    vmem = pl.BlockSpec(memory_space=pltpu.VMEM)
    return pl.pallas_call(
        kernel,
        out_shape=jax.ShapeDtypeStruct(right_side.shape, jnp.float32),
        in_specs=[vmem] * 3,
        out_specs=vmem,
        scratch_shapes=scratch,
        compiler_params=pltpu.CompilerParams(
            collective_id=0, has_side_effects=True, vmem_limit_bytes=56 * 2**20
        ),
    )(right_side, stiffness, reaction)


def solution(mesh):
    in_specs = (P(None, "grp", "brick", None), P("grp", "brick", None), P("grp", "brick", None))
    out_specs = P(None, "grp", "brick", None)
    return jax.shard_map(
        on_device, mesh=mesh, in_specs=in_specs, out_specs=out_specs, check_vma=False
    )
```

```python
import jax
import jax.numpy as jnp
from jax import lax
from jax.experimental import pallas as pl
from jax.experimental.pallas import tpu as pltpu
from jax.sharding import PartitionSpec as P

BETA = 1.0
THETA = 1.5
DELTA = 1.0
SIGMA = 1.5
HX = 6
HY = 8
LANES = 128
DIRS = [(a, b) for a in (-1, 0, 1) for b in (-1, 0, 1) if (a, b) != (0, 0)]


def rate_list():
    rates = [1.0 / SIGMA]
    for number in range(3):
        rates.append(1.0 / (2.0 * SIGMA - rates[-1]))
    return rates


def round8(number):
    return -(-number // 8) * 8


def lane(rows):
    return lax.broadcasted_iota(jnp.int32, (rows, LANES), 1)


def roll(value, shift):
    return pltpu.roll(value, shift % LANES, 1)


def pack(values, group):
    if group == 1:
        return values[0]
    place = lane(values[0].shape[0]) % group
    out = values[0]
    for t in range(1, len(values)):
        out = jnp.where(place == t, values[t], out)
    return out


def unpack(value, group, t):
    if group == 1:
        return value
    out = jnp.where(lane(value.shape[0]) % group == t, value, 0.0)
    if t:
        out = roll(out, -t)
    shift = 1
    while shift < group:
        out = out + roll(out, shift)
        shift *= 2
    return out


def halve_lanes(value, group):
    first = lane(value.shape[0]) % (2 * group) < group
    return value + jnp.where(first, roll(value, -group), roll(value, group))


def rows_loop(start, count, most, body, carry=None):
    each = max(n for n in range(1, most + 1) if count % n == 0)
    if count == each:
        return body([start + t for t in range(each)], carry)

    def step(n, carry):
        out = body([start + n * each + t for t in range(each)], carry)
        return 0 if out is None else out

    return lax.fori_loop(0, count // each, step, 0 if carry is None else carry)


class Exchange:
    def __init__(self, size, group, packed, widths):
        self.size, self.group, self.packed, self.widths = size, group, packed, widths
        self.blocks = size // group
        self.offs = [sum(widths[:n]) for n in range(len(widths))]
        self.width = sum(widths)
        self.side_rows = round8(self.blocks * self.width)
        self.corner_rows = round8(packed * self.width)
        self.front_rows = round8(packed * len(widths) * size)

    def scratch(self):
        both = [
            pltpu.VMEM((2, self.front_rows, LANES), jnp.float32),
            pltpu.VMEM((2, self.side_rows, LANES), jnp.float32),
            pltpu.VMEM((4, self.corner_rows, LANES), jnp.float32),
        ]
        return both + both + [pltpu.SemaphoreType.DMA((8,)), pltpu.SemaphoreType.DMA((8,))]

    def bind(self, refs, where):
        self.sx, self.sy, self.sc, self.rx, self.ry, self.rc, self.ssem, self.rsem = refs
        self.where = where

    def corner(self, ex, ey):
        rows, at = [], 0
        for j in range(self.packed):
            for field, width in enumerate(self.widths):
                if ex == ey and self.group == 1:
                    width -= j + 1 if ex < 0 else self.packed - j
                if width > 0:
                    rows.append((j, field, width, at))
                    at += width
        return rows, round8(at)

    def copy(self, ex, ey):
        g, b, _ = self.where
        if ey == 0:
            side = 0 if ex < 0 else 1
            src, dst = self.sx.at[side], self.rx.at[1 - side]
        elif ex == 0:
            side = 0 if ey < 0 else 1
            src, dst = self.sy.at[side], self.ry.at[1 - side]
        else:
            side = (1 if ex > 0 else 0) * 2 + (1 if ey > 0 else 0)
            rows = pl.ds(0, self.corner(ex, ey)[1])
            src, dst = self.sc.at[side, rows], self.rc.at[3 - side, rows]
        return pltpu.make_async_remote_copy(
            src_ref=src,
            dst_ref=dst,
            send_sem=self.ssem.at[DIRS.index((ex, ey))],
            recv_sem=self.rsem.at[DIRS.index((-ex, -ey))],
            device_id=(g + ex, b + ey),
            device_id_type=pl.DeviceIdType.MESH,
        )

    def stage(self, get):
        size, group, last = self.size, self.group, self.blocks - self.packed

        def load(field, j, r0, count):
            return pack([get(field, j * group + t, r0, count) for t in range(group)], group)

        for j in range(self.blocks):
            for field, width in enumerate(self.widths):
                for side in (0, 1):
                    value = load(field, j, 0 if side == 0 else size - width, width)
                    at = j * self.width + self.offs[field]
                    self.sy[side, at : at + width, :] = value
        for ex in (-1, 1):
            for ey in (-1, 1):
                side = (1 if ex > 0 else 0) * 2 + (1 if ey > 0 else 0)
                for j, field, width, at in self.corner(ex, ey)[0]:
                    r0 = 0 if ey < 0 else size - width
                    value = load(field, j if ex < 0 else last + j, r0, width)
                    self.sc[side, at : at + width, :] = value
        for side in (0, 1):
            for j in range(self.packed):
                for field in range(len(self.widths)):
                    at = (j * len(self.widths) + field) * size
                    value = load(field, j if side == 0 else last + j, 0, size)
                    self.sx[side, at : at + size, :] = value

    def start(self):
        exists = self.where[2]
        for d in DIRS:
            @pl.when(exists[d])
            def _(d=d):
                self.copy(*d).start()

    def finish_send(self):
        exists = self.where[2]
        for d in DIRS:
            @pl.when(exists[d])
            def _(d=d):
                self.copy(*d).wait_send()

    def finish(self, put):
        exists = self.where[2]
        size, group = self.size, self.group

        def spread_rows(value, x0, field, y0):
            for t in range(group):
                put(field, x0 + t, y0, unpack(value, group, t))

        for d in DIRS:
            @pl.when(exists[d])
            def _(d=d):
                dx, dy = d
                self.copy(-dx, -dy).wait_recv()
                xside, yside = (0 if dx < 0 else 1), (0 if dy < 0 else 1)
                base = {-1: -self.packed * group, 0: 0, 1: size}[dx]
                if dx and dy:
                    for j, field, width, at in self.corner(-dx, -dy)[0]:
                        value = self.rc[2 * xside + yside, at : at + width, :]
                        y0 = -width if dy < 0 else size
                        spread_rows(value, base + j * group, field, y0)
                    return
                for j in range(self.packed if dx else self.blocks):
                    for field, width in enumerate(self.widths):
                        if dy == 0:
                            at = (j * len(self.widths) + field) * size
                            value, y0 = self.rx[xside, at : at + size, :], 0
                        else:
                            at = j * self.width + self.offs[field]
                            value = self.ry[yside, at : at + width, :]
                            y0 = -width if dy < 0 else size
                        spread_rows(value, base + j * group, field, y0)


class Level:
    NAMES = ("f", "xa", "xb", "p")
    COEFF = ("k", "rea", "kx", "ky", "kz", "kzm", "dg", "inv")

    def __init__(self, number, xsize, ysize, window):
        self.number, self.xsize, self.ysize, self.window = number, xsize, ysize, window
        self.group = 2**number
        self.scale = 0.25**number
        self.shape = (xsize + 2 * HX, round8(ysize) + 2 * HY, LANES)

    def scratch(self):
        f32 = jnp.float32
        return [pltpu.VMEM((3,) + self.shape, f32) for _ in self.NAMES] + [
            pltpu.VMEM(self.shape, f32) for _ in self.COEFF
        ]

    def bind(self, refs):
        for name, ref in zip(self.NAMES + self.COEFF, refs):
            setattr(self, name, ref)

    def clear(self):
        zero = jnp.zeros(self.shape[1:], jnp.float32)

        def body(i, carry):
            for name in self.NAMES:
                for c in range(3):
                    getattr(self, name)[c, i] = zero
            for name in self.COEFF:
                getattr(self, name)[i] = zero
            return carry

        lax.fori_loop(0, self.shape[0], body, 0)

    def prepare(self, halo, gx0, gy0, xcount, ycount):
        w0, wn = self.window
        z = self.group
        s = self.scale
        lanes = lane(wn)
        first, last = lanes < z, lanes >= LANES - z
        rows = lax.broadcasted_iota(jnp.int32, (wn, LANES), 0) + (w0 - HY) + gy0
        inside_y = (rows >= 0) & (rows < ycount)
        w = slice(w0, w0 + wn)
        wm = slice(w0 - 1, w0 + wn - 1)
        wp = slice(w0 + 1, w0 + wn + 1)

        def one(i):
            centre = self.k[i, w, :]
            behind = self.k[i, wm, :]
            ahead = self.k[i, wp, :]
            up, down = self.k[i + 1, w, :], self.k[i - 1, w, :]
            zp = jnp.where(last, 0.0, roll(centre, -z))
            zm = jnp.where(first, 0.0, roll(centre, z))
            total = 3.0 * centre + 0.5 * ((up + down) + (ahead + behind) + (zp + zm))
            diag = s * total + self.rea[i, w, :]
            row = gx0 + i - HX
            inside = inside_y & (row >= 0) & (row < xcount)
            return (
                diag,
                (0.5 * s) * (centre + up),
                (0.5 * s) * (behind + centre),
                jnp.where(last, 0.0, (0.5 * s) * (centre + zp)),
                jnp.where(first, 0.0, (0.5 * s) * (centre + zm)),
                jnp.where(inside, 1.0 / (diag + 2.0 * BETA * s), 0.0),
            )

        def body(rows, carry):
            for i, values in [(i, one(i)) for i in rows]:
                self.dg[i, w, :] = values[0]
                self.kx[i, w, :] = values[1]
                self.ky[i, wm, :] = values[2]
                self.kz[i, w, :] = values[3]
                self.kzm[i, w, :] = values[4]
                self.inv[i, w, :] = values[5]

        rows_loop(HX - halo, self.xsize + 2 * halo, 4, body)

    def sweep(self, src, halo, window, consume):
        w0, wn = window
        z = self.group
        bs = BETA * self.scale
        lanes = lane(wn)
        first, last = lanes < z, lanes >= LANES - z
        w = slice(w0, w0 + wn)
        wm = slice(w0 - 1, w0 + wn - 1)
        wp = slice(w0 + 1, w0 + wn + 1)

        def scaled(value):
            return value if bs == 1.0 else bs * value

        def flat(i, rows, rows_next):
            total = src[0, i + 1, rows, :] - src[0, i, rows, :]
            return total + (src[1, i, rows_next, :] - src[1, i, rows, :])

        def div(part, uz, ahead):
            return scaled(part + (jnp.where(last, 0.0, ahead) - uz))

        def one(i, before):
            u = [src[c, i, w, :] for c in range(3)]
            ahead = [roll(u[c], -z) for c in range(3)]
            behind = [roll(u[c], z) for c in range(3)]
            part = flat(i, w, wp)
            here = div(part, u[2], ahead[2])
            side_z = src[2, i, wm, :]
            beside = div(flat(i, wm, w), side_z, roll(side_z, -z))
            under = scaled(u[2] + jnp.where(first, 0.0, roll(part - u[2], z)))
            gradients = (before, beside, under)
            kxp, kxm = self.kx[i, w, :], self.kx[i - 1, w, :]
            kyp, kym = self.ky[i, w, :], self.ky[i, wm, :]
            kzp, kzm = self.kz[i, w, :], self.kzm[i, w, :]
            dg = self.dg[i, w, :]
            out = []
            for c in range(3):
                near = kxp * src[c, i + 1, w, :] + kxm * src[c, i - 1, w, :]
                near = near + (kyp * src[c, i, wp, :] + kym * src[c, i, wm, :])
                near = near + (kzp * ahead[c] + kzm * behind[c])
                out.append(dg * u[c] - near + (gradients[c] - here))
            return consume(i, w, u, out), here

        def body(rows, before):
            stores = []
            for i in rows:
                more, before = one(i, before)
                stores += more
            for ref, index, value in stores:
                ref[index] = value
            return before

        lo = HX - halo
        uz = src[2, lo - 1, w, :]
        before = div(flat(lo - 1, w, wp), uz, roll(uz, -z))
        most = 4 if self.number == 0 else 7
        rows_loop(lo, self.xsize + 2 * halo, most, body, before)

    def step(self, src, dst, halo, number, window=None, out=None):
        rates = rate_list()

        def consume(i, w, u, au):
            gain = 1.0 / THETA if number == 0 else 2.0 * rates[number] / DELTA
            inv = gain * self.inv[i, w, :]
            stores = []
            for c in range(3):
                p = inv * (self.f[c, i, w, :] - au[c])
                if number:
                    p = p + rates[number] * rates[number - 1] * self.p[c, i, w, :]
                at = (c, i, w, slice(None))
                if number < 3:
                    stores.append((self.p, at, p))
                if out is not None:
                    stores.append((out, (c, i - HX), u[c] + p))
                else:
                    stores.append((dst, at, u[c] + p))
            return stores

        self.sweep(src, halo, window or self.window, consume)

    def first_direction(self, halo):
        w0, wn = self.window
        w = slice(w0, w0 + wn)

        def body(rows, carry):
            stores = []
            for i in rows:
                inv = (1.0 / THETA) * self.inv[i, w, :]
                stores += [(i, c, inv * self.f[c, i, w, :]) for c in range(3)]
            for i, c, p in stores:
                self.p[c, i, w, :] = p
                self.xa[c, i, w, :] = p

        rows_loop(HX - halo, self.xsize + 2 * halo, 4, body)

    def smooth_down(self, halo):
        self.step(self.xa, self.xb, max(halo - 1, 0), 1)
        self.step(self.xb, self.xa, max(halo - 2, 0), 2)
        self.step(self.xa, self.xb, max(halo - 3, 0), 3)

    def residual(self):
        def consume(i, w, u, au):
            at = [(c, i, w, slice(None)) for c in range(3)]
            return [(self.p, at[c], self.f[c, i, w, :] - au[c]) for c in range(3)]

        self.sweep(self.xb, 0, (HY, round8(self.ysize)), consume)

    def add_grown(self, coarse, xoff, yoff, temp):
        w0, wn = self.window
        w = slice(w0, w0 + wn)
        half = wn // 2
        rows = pl.ds(yoff + HY + (w0 - HY) // 2, half)

        def body(js, carry):
            for n, j in enumerate(js):
                for c in range(3):
                    value = coarse[c, j + (xoff + HX - 2), rows, :]
                    temp[3 * n + c, pl.ds(0, half, stride=2), :] = value
                    temp[3 * n + c, pl.ds(1, half, stride=2), :] = value
            for n, j in enumerate(js):
                for c in range(3):
                    grown = temp[3 * n + c, 0:wn, :]
                    for t in range(2):
                        i = HX - 4 + 2 * j + t
                        self.xa[c, i, w, :] = self.xb[c, i, w, :] + grown

        rows_loop(0, (self.xsize + 8) // 2, 4, body)


def shrink_fields(fine, pairs):
    half = fine.ysize // 2

    def body(js, carry):
        values = []
        for j in js:
            for load, store in pairs:
                total = load(2 * j, 0, half) + load(2 * j, 1, half)
                total = total + (load(2 * j + 1, 0, half) + load(2 * j + 1, 1, half))
                values.append((store, j, 0.125 * halve_lanes(total, fine.group)))
        for store, j, value in values:
            store(j, value)

    rows_loop(0, fine.xsize // 2, 4, body)


def plan(xsize, ysize, groups, bricks):
    levels = []
    for number in range(3):
        size = ysize >> number
        levels.append(Level(number, xsize >> number, size, (HY - 4, round8(size + 8))))
    coarse = (xsize >> 3) * groups, (ysize >> 3) * bricks
    levels.append(Level(3, coarse[0], coarse[1], (HY, round8(coarse[1]))))
    size = xsize
    exchanges = dict(
        c0=Exchange(size, 1, 5, (4, 5)),
        f0=Exchange(size, 1, 4, (4, 4, 4)),
        c1=Exchange(size // 2, 2, 3, (4, 5)),
        c2=Exchange(size // 4, 4, 1, (4, 4)),
        f1=Exchange(size // 2, 2, 2, (4, 4, 4)),
        f2=Exchange(size // 4, 4, 1, (4,) * 6),
        x0=Exchange(size, 1, 4, (4, 4, 4)),
        x1=Exchange(size // 2, 2, 2, (4, 4, 4)),
        x2=Exchange(size // 4, 4, 1, (4, 4, 4)),
        y2=Exchange(size // 4, 4, 1, (2, 2, 2)),
        y1=Exchange(size // 2, 2, 1, (2, 2, 2)),
    )
    return levels, exchanges


def cycle(groups, bricks, xsize, ysize, f_in, k_in, rea_in, out, *scratch):
    levels, exchanges = plan(xsize, ysize, groups, bricks)
    devices = groups * bricks
    g, b = lax.axis_index("grp"), lax.axis_index("brick")
    me = g * bricks + b
    exists = {}
    for dx, dy in DIRS:
        good = None
        for d, at, count in ((dx, g, groups), (dy, b, bricks)):
            if d:
                test = at > 0 if d < 0 else at < count - 1
                good = test if good is None else good & test
        exists[(dx, dy)] = good
    scratch = list(scratch)

    def take(count):
        got = scratch[:count]
        del scratch[:count]
        return got

    for level in levels:
        level.bind(take(12))
    for name in exchanges:
        exchanges[name].bind(take(8), (g, b, exists))
    temp, slot, slots, slot_send, slot_recv = take(5)
    ex = exchanges
    l0, l1, l2, l3 = levels

    barrier = pltpu.get_barrier_semaphore()

    def partner(n):
        other = (me + n) % devices
        return other // bricks, other % bricks

    def greet(n, carry):
        pl.semaphore_signal(
            barrier, inc=1, device_id=partner(n), device_id_type=pl.DeviceIdType.MESH
        )
        return carry

    lax.fori_loop(1, devices, greet, 0)

    def get_coeff(field, i, r0, count):
        return (rea_in, k_in)[field][i, r0 : r0 + count, :]

    def get_source(field, i, r0, count):
        return f_in[field, i, r0 : r0 + count, :]

    ex["c0"].stage(get_coeff)
    pl.semaphore_wait(barrier, devices - 1)
    ex["c0"].start()
    ex["f0"].stage(get_source)
    ex["f0"].start()

    for level in levels:
        level.clear()

    def load_own(i, carry):
        own = slice(HY, HY + ysize)
        for c in range(3):
            l0.f[c, HX + i, own, :] = f_in[c, i]
        l0.k[HX + i, own, :] = k_in[i]
        l0.rea[HX + i, own, :] = rea_in[i]
        return carry

    lax.fori_loop(0, xsize, load_own, 0)

    def shrink_pair(ref, target):
        def load(x, y, count):
            return ref[HX + x, pl.ds(HY + y, count, stride=2), :]

        def store(j, value):
            target[HX + j, HY : HY + value.shape[0], :] = value

        return load, store

    for fine, coarse in ((l0, l1), (l1, l2)):
        pairs = [shrink_pair(fine.k, coarse.k), shrink_pair(fine.rea, coarse.rea)]
        shrink_fields(fine, pairs)

    def getter(*refs):
        def get(field, i, r0, count):
            ref, c = refs[field]
            rows = slice(HY + r0, HY + r0 + count)
            return ref[HX + i, rows, :] if c is None else ref[c, HX + i, rows, :]

        return get

    def putter(*refs):
        def put(field, i, r0, value):
            ref, c = refs[field]
            rows = slice(HY + r0, HY + r0 + value.shape[0])
            if c is None:
                ref[HX + i, rows, :] = value
            else:
                ref[c, HX + i, rows, :] = value

        return put

    def three(ref):
        return tuple((ref, c) for c in range(3))

    def own_prepare(level, halo):
        xs, ys = level.xsize, level.ysize
        level.prepare(halo, g * xs, b * ys, xs * groups, ys * bricks)

    ex["c1"].stage(getter((l1.rea, None), (l1.k, None)))
    ex["c2"].stage(getter((l2.rea, None), (l2.k, None)))
    ex["c0"].finish(putter((l0.rea, None), (l0.k, None)))

    def shrink_residual(fine, coarse):
        pairs = [shrink_pair(fine.p.at[c], coarse.f.at[c]) for c in range(3)]
        shrink_fields(fine, pairs)

    own_prepare(l0, 4)
    ex["f0"].finish(putter(*three(l0.f)))
    ex["c1"].start()
    ex["c2"].start()
    l0.first_direction(4)
    l0.smooth_down(4)
    l0.residual()
    shrink_residual(l0, l1)

    ex["f1"].stage(getter(*three(l1.f)))
    ex["f1"].start()
    ex["x0"].stage(getter(*three(l0.xb)))
    ex["c1"].finish(putter((l1.rea, None), (l1.k, None)))
    ex["c2"].finish(putter((l2.rea, None), (l2.k, None)))
    own_prepare(l1, 4)
    own_prepare(l2, 4)
    ex["f1"].finish(putter(*three(l1.f)))
    l1.first_direction(4)
    l1.smooth_down(4)
    l1.residual()
    shrink_residual(l1, l2)

    l2.first_direction(0)
    ex["f2"].stage(getter(*three(l2.f), *three(l2.p)))
    ex["f2"].start()
    ex["x1"].stage(getter(*three(l1.xb)))

    def put_f2(field, i, r0, value):
        putter(*three(l2.f), *three(l2.p))(field, i, r0, value)
        if field >= 3:
            putter(*three(l2.xa))(field - 3, i, r0, value)

    for name in ("c0", "f0", "c1", "c2", "f1"):
        ex[name].finish_send()
    ex["f2"].finish(put_f2)
    l2.smooth_down(4)
    ex["x2"].stage(getter(*three(l2.xb)))
    ex["x2"].start()
    l2.residual()

    def load_fine(field, x, y):
        rows = slice(HY + y, HY + y + 1)
        if field < 3:
            return l2.p[field, HX + x, rows, :]
        return (l2.rea if field == 3 else l2.k)[HX + x, rows, :]

    slot[...] = jnp.zeros_like(slot)
    for field in range(5):
        values = []
        for x in range(2):
            for y in range(2):
                total = load_fine(field, 2 * x, 2 * y) + load_fine(field, 2 * x, 2 * y + 1)
                total = total + load_fine(field, 2 * x + 1, 2 * y)
                total = total + load_fine(field, 2 * x + 1, 2 * y + 1)
                values.append(0.125 * halve_lanes(total, 4))
        slot[field : field + 1, :] = pack(values, 8)

    def gather_copy(n):
        return pltpu.make_async_remote_copy(
            src_ref=slot,
            dst_ref=slots.at[pl.ds(me * 8, 8)],
            send_sem=slot_send.at[n],
            recv_sem=slot_recv.at[me],
            device_id=partner(n),
            device_id_type=pl.DeviceIdType.MESH,
        )

    def send_slot(n, carry):
        gather_copy(n).start()
        return carry

    lax.fori_loop(1, devices, send_slot, 0)

    slots[pl.ds(pl.multiple_of(me * 8, 8), 8), :] = slot[...]

    def receive(n, carry):
        owner = (me + n) % devices
        pltpu.make_async_remote_copy(
            src_ref=slot,
            dst_ref=slots.at[pl.ds(owner * 8, 8)],
            send_sem=slot_send.at[n],
            recv_sem=slot_recv.at[owner],
            device_id=partner(n),
            device_id_type=pl.DeviceIdType.MESH,
        ).wait_recv()
        return carry

    lax.fori_loop(1, devices, receive, 0)
    ex["x1"].start()
    ex["x0"].start()
    for og in range(groups):
        for field in range(5):
            value = slots[pl.ds(og * bricks * 8 + field, bricks, stride=8), :]
            for x in range(2):
                for y in range(2):
                    line = unpack(value, 8, 2 * x + y)
                    row, cols = HX + 2 * og + x, pl.ds(HY + y, bricks, stride=2)
                    if field < 3:
                        l3.f[field, row, cols, :] = line
                    else:
                        (l3.rea if field == 3 else l3.k)[row, cols, :] = line
    l3.prepare(0, 0, 0, l3.xsize, l3.ysize)
    edge = slice(l3.window[0], l3.window[0] + l3.window[1])
    l3.kx[HX - 1, edge, :] = (0.5 * l3.scale) * l3.k[HX, edge, :]
    l3.first_direction(0)
    l3.smooth_down(0)

    ex["x2"].finish(putter(*three(l2.xb)))
    l2.add_grown(l3.xb, g * (xsize // 8), b * (ysize // 8), temp)
    up(l2)
    ex["y2"].stage(getter(*three(l2.xa)))
    ex["y2"].start()
    ex["x1"].finish(putter(*three(l1.xb)))

    def sent(n, carry):
        gather_copy(n).wait_send()
        return carry

    lax.fori_loop(1, devices, sent, 0)
    for name in ("f2", "x1", "x2"):
        ex[name].finish_send()
    ex["y2"].finish(putter(*three(l2.xa)))
    l1.add_grown(l2.xa, 0, 0, temp)
    up(l1)
    ex["y1"].stage(getter(*three(l1.xa)))
    ex["y1"].start()
    ex["x0"].finish(putter(*three(l0.xb)))
    ex["y2"].finish_send()
    ex["y1"].finish(putter(*three(l1.xa)))
    l0.add_grown(l1.xa, 0, 0, temp)
    up(l0, out)

    ex["x0"].finish_send()
    ex["y1"].finish_send()


def up(level, out=None):
    level.step(level.xa, level.xb, 3, 0)
    level.step(level.xb, level.xa, 2, 1)
    level.step(level.xa, level.xb, 1, 2)
    level.step(level.xb, level.xa, 0, 3, (HY, round8(level.ysize)), out)


def on_device(right_side, stiffness, reaction):
    groups, bricks = lax.axis_size("grp"), lax.axis_size("brick")
    _, xsize, ysize, _ = right_side.shape
    levels, exchanges = plan(xsize, ysize, groups, bricks)
    devices = groups * bricks
    scratch = []
    for level in levels:
        scratch += level.scratch()
    for name in exchanges:
        scratch += exchanges[name].scratch()
    scratch += [
        pltpu.VMEM((12, 32, LANES), jnp.float32),
        pltpu.VMEM((8, LANES), jnp.float32),
        pltpu.VMEM((8 * devices, LANES), jnp.float32),
        pltpu.SemaphoreType.DMA((devices,)),
        pltpu.SemaphoreType.DMA((devices,)),
    ]

    def kernel(*refs):
        cycle(groups, bricks, xsize, ysize, *refs)

    vmem = pl.BlockSpec(memory_space=pltpu.VMEM)
    return pl.pallas_call(
        kernel,
        out_shape=jax.ShapeDtypeStruct(right_side.shape, jnp.float32),
        in_specs=[vmem] * 3,
        out_specs=vmem,
        scratch_shapes=scratch,
        compiler_params=pltpu.CompilerParams(
            collective_id=0, has_side_effects=True, vmem_limit_bytes=56 * 2**20
        ),
    )(right_side, stiffness, reaction)


def solution(mesh):
    in_specs = (P(None, "grp", "brick", None), P("grp", "brick", None), P("grp", "brick", None))
    out_specs = P(None, "grp", "brick", None)
    return jax.shard_map(
        on_device, mesh=mesh, in_specs=in_specs, out_specs=out_specs, check_vma=False
    )
```

```python
import jax
import jax.numpy as jnp
from jax import lax
from jax.experimental import pallas as pl
from jax.experimental.pallas import tpu as pltpu
from jax.sharding import PartitionSpec as P

BETA = 1.0
THETA = 1.5
DELTA = 1.0
SIGMA = 1.5
HX = 6
HY = 8
LANES = 128
DIRS = [(a, b) for a in (-1, 0, 1) for b in (-1, 0, 1) if (a, b) != (0, 0)]
START = sorted(DIRS, key=lambda d: (d[1] == 0, d[0] != 0))
FINISH = START[::-1]


def rate_list():
    rates = [1.0 / SIGMA]
    for number in range(3):
        rates.append(1.0 / (2.0 * SIGMA - rates[-1]))
    return rates


def round8(number):
    return -(-number // 8) * 8


def lane(rows):
    return lax.broadcasted_iota(jnp.int32, (rows, LANES), 1)


def roll(value, shift):
    return pltpu.roll(value, shift % LANES, 1)


def pack(values, group):
    if group == 1:
        return values[0]
    place = lane(values[0].shape[0]) % group
    out = values[0]
    for t in range(1, len(values)):
        out = jnp.where(place == t, values[t], out)
    return out


def unpack(value, group, t):
    if group == 1:
        return value
    out = jnp.where(lane(value.shape[0]) % group == t, value, 0.0)
    if t:
        out = roll(out, -t)
    shift = 1
    while shift < group:
        out = out + roll(out, shift)
        shift *= 2
    return out


def halve_lanes(value, group):
    first = lane(value.shape[0]) % (2 * group) < group
    return value + jnp.where(first, roll(value, -group), roll(value, group))


def rows_loop(start, count, most, body, carry=None):
    each = max(n for n in range(1, most + 1) if count % n == 0)
    if count == each:
        return body([start + t for t in range(each)], carry)

    def step(n, carry):
        out = body([start + n * each + t for t in range(each)], carry)
        return 0 if out is None else out

    return lax.fori_loop(0, count // each, step, 0 if carry is None else carry)


class Exchange:
    def __init__(self, size, group, packed, widths):
        self.size, self.group, self.packed, self.widths = size, group, packed, widths
        self.blocks = size // group
        self.offs = [sum(widths[:n]) for n in range(len(widths))]
        self.width = sum(widths)
        self.side_rows = round8(self.blocks * self.width)
        self.corner_rows = round8(packed * self.width)
        self.front_rows = round8(packed * len(widths) * size)

    def scratch(self):
        both = [
            pltpu.VMEM((2, self.front_rows, LANES), jnp.float32),
            pltpu.VMEM((2, self.side_rows, LANES), jnp.float32),
            pltpu.VMEM((4, self.corner_rows, LANES), jnp.float32),
        ]
        return both + both + [pltpu.SemaphoreType.DMA((8,)), pltpu.SemaphoreType.DMA((8,))]

    def bind(self, refs, where):
        self.sx, self.sy, self.sc, self.rx, self.ry, self.rc, self.ssem, self.rsem = refs
        self.where = where

    def corner(self, ex, ey):
        rows, at = [], 0
        for j in range(self.packed):
            for field, width in enumerate(self.widths):
                if ex == ey and self.group == 1:
                    width -= j + 1 if ex < 0 else self.packed - j
                if width > 0:
                    rows.append((j, field, width, at))
                    at += width
        return rows, round8(at)

    def copy(self, ex, ey):
        g, b, _ = self.where
        if ey == 0:
            side = 0 if ex < 0 else 1
            src, dst = self.sx.at[side], self.rx.at[1 - side]
        elif ex == 0:
            side = 0 if ey < 0 else 1
            src, dst = self.sy.at[side], self.ry.at[1 - side]
        else:
            side = (1 if ex > 0 else 0) * 2 + (1 if ey > 0 else 0)
            rows = pl.ds(0, self.corner(ex, ey)[1])
            src, dst = self.sc.at[side, rows], self.rc.at[3 - side, rows]
        return pltpu.make_async_remote_copy(
            src_ref=src,
            dst_ref=dst,
            send_sem=self.ssem.at[DIRS.index((ex, ey))],
            recv_sem=self.rsem.at[DIRS.index((-ex, -ey))],
            device_id=(g + ex, b + ey),
            device_id_type=pl.DeviceIdType.MESH,
        )

    def stage(self, get):
        size, group, last = self.size, self.group, self.blocks - self.packed

        def load(field, j, r0, count):
            return pack([get(field, j * group + t, r0, count) for t in range(group)], group)

        for j in range(self.blocks):
            for field, width in enumerate(self.widths):
                for side in (0, 1):
                    value = load(field, j, 0 if side == 0 else size - width, width)
                    at = j * self.width + self.offs[field]
                    self.sy[side, at : at + width, :] = value
        for ex in (-1, 1):
            for ey in (-1, 1):
                side = (1 if ex > 0 else 0) * 2 + (1 if ey > 0 else 0)
                for j, field, width, at in self.corner(ex, ey)[0]:
                    r0 = 0 if ey < 0 else size - width
                    value = load(field, j if ex < 0 else last + j, r0, width)
                    self.sc[side, at : at + width, :] = value
        for side in (0, 1):
            for j in range(self.packed):
                for field in range(len(self.widths)):
                    at = (j * len(self.widths) + field) * size
                    value = load(field, j if side == 0 else last + j, 0, size)
                    self.sx[side, at : at + size, :] = value

    def start(self):
        exists = self.where[2]
        for d in START:
            @pl.when(exists[d])
            def _(d=d):
                self.copy(*d).start()

    def finish_send(self):
        exists = self.where[2]
        for d in DIRS:
            @pl.when(exists[d])
            def _(d=d):
                self.copy(*d).wait_send()

    def finish(self, put):
        exists = self.where[2]
        size, group = self.size, self.group

        def spread_rows(value, x0, field, y0):
            for t in range(group):
                put(field, x0 + t, y0, unpack(value, group, t))

        for d in FINISH:
            @pl.when(exists[d])
            def _(d=d):
                dx, dy = d
                self.copy(-dx, -dy).wait_recv()
                xside, yside = (0 if dx < 0 else 1), (0 if dy < 0 else 1)
                base = {-1: -self.packed * group, 0: 0, 1: size}[dx]
                if dx and dy:
                    for j, field, width, at in self.corner(-dx, -dy)[0]:
                        value = self.rc[2 * xside + yside, at : at + width, :]
                        y0 = -width if dy < 0 else size
                        spread_rows(value, base + j * group, field, y0)
                    return
                for j in range(self.packed if dx else self.blocks):
                    for field, width in enumerate(self.widths):
                        if dy == 0:
                            at = (j * len(self.widths) + field) * size
                            value, y0 = self.rx[xside, at : at + size, :], 0
                        else:
                            at = j * self.width + self.offs[field]
                            value = self.ry[yside, at : at + width, :]
                            y0 = -width if dy < 0 else size
                        spread_rows(value, base + j * group, field, y0)


class Level:
    NAMES = ("f", "xa", "xb", "p")
    COEFF = ("k", "rea", "kx", "ky", "kz", "kzm", "dg", "inv")

    def __init__(self, number, xsize, ysize, window):
        self.number, self.xsize, self.ysize, self.window = number, xsize, ysize, window
        self.group = 2**number
        self.scale = 0.25**number
        self.shape = (xsize + 2 * HX, round8(ysize) + 2 * HY, LANES)

    def scratch(self):
        f32 = jnp.float32
        return [pltpu.VMEM((3,) + self.shape, f32) for _ in self.NAMES] + [
            pltpu.VMEM(self.shape, f32) for _ in self.COEFF
        ]

    def bind(self, refs):
        for name, ref in zip(self.NAMES + self.COEFF, refs):
            setattr(self, name, ref)

    def clear(self):
        zero = jnp.zeros(self.shape[1:], jnp.float32)

        def body(i, carry):
            for name in self.NAMES:
                for c in range(3):
                    getattr(self, name)[c, i] = zero
            for name in self.COEFF:
                getattr(self, name)[i] = zero
            return carry

        lax.fori_loop(0, self.shape[0], body, 0)

    def prepare(self, halo, gx0, gy0, xcount, ycount):
        w0, wn = self.window
        z = self.group
        s = self.scale
        lanes = lane(wn)
        first, last = lanes < z, lanes >= LANES - z
        rows = lax.broadcasted_iota(jnp.int32, (wn, LANES), 0) + (w0 - HY) + gy0
        inside_y = (rows >= 0) & (rows < ycount)
        w = slice(w0, w0 + wn)
        wm = slice(w0 - 1, w0 + wn - 1)
        wp = slice(w0 + 1, w0 + wn + 1)

        def one(i):
            centre = self.k[i, w, :]
            behind = self.k[i, wm, :]
            ahead = self.k[i, wp, :]
            up, down = self.k[i + 1, w, :], self.k[i - 1, w, :]
            zp = jnp.where(last, 0.0, roll(centre, -z))
            zm = jnp.where(first, 0.0, roll(centre, z))
            total = 3.0 * centre + 0.5 * ((up + down) + (ahead + behind) + (zp + zm))
            diag = s * total + self.rea[i, w, :]
            row = gx0 + i - HX
            inside = inside_y & (row >= 0) & (row < xcount)
            return (
                diag,
                (0.5 * s) * (centre + up),
                (0.5 * s) * (behind + centre),
                jnp.where(last, 0.0, (0.5 * s) * (centre + zp)),
                jnp.where(first, 0.0, (0.5 * s) * (centre + zm)),
                jnp.where(inside, 1.0 / (diag + 2.0 * BETA * s), 0.0),
            )

        def body(rows, carry):
            for i, values in [(i, one(i)) for i in rows]:
                self.dg[i, w, :] = values[0]
                self.kx[i, w, :] = values[1]
                self.ky[i, wm, :] = values[2]
                self.kz[i, w, :] = values[3]
                self.kzm[i, w, :] = values[4]
                self.inv[i, w, :] = values[5]

        rows_loop(HX - halo, self.xsize + 2 * halo, 4, body)

    def sweep(self, src, halo, window, consume):
        w0, wn = window
        z = self.group
        bs = BETA * self.scale
        lanes = lane(wn)
        first, last = lanes < z, lanes >= LANES - z
        w = slice(w0, w0 + wn)
        wm = slice(w0 - 1, w0 + wn - 1)
        wp = slice(w0 + 1, w0 + wn + 1)

        def scaled(value):
            return value if bs == 1.0 else bs * value

        def flat(i, rows, rows_next):
            total = src[0, i + 1, rows, :] - src[0, i, rows, :]
            return total + (src[1, i, rows_next, :] - src[1, i, rows, :])

        def div(part, uz, ahead):
            return scaled(part + (jnp.where(last, 0.0, ahead) - uz))

        def one(i, before):
            u = [src[c, i, w, :] for c in range(3)]
            ahead = [roll(u[c], -z) for c in range(3)]
            behind = [roll(u[c], z) for c in range(3)]
            part = flat(i, w, wp)
            here = div(part, u[2], ahead[2])
            side_z = src[2, i, wm, :]
            beside = div(flat(i, wm, w), side_z, roll(side_z, -z))
            under = scaled(u[2] + jnp.where(first, 0.0, roll(part - u[2], z)))
            gradients = (before, beside, under)
            kxp, kxm = self.kx[i, w, :], self.kx[i - 1, w, :]
            kyp, kym = self.ky[i, w, :], self.ky[i, wm, :]
            kzp, kzm = self.kz[i, w, :], self.kzm[i, w, :]
            dg = self.dg[i, w, :]
            out = []
            for c in range(3):
                near = kxp * src[c, i + 1, w, :] + kxm * src[c, i - 1, w, :]
                near = near + (kyp * src[c, i, wp, :] + kym * src[c, i, wm, :])
                near = near + (kzp * ahead[c] + kzm * behind[c])
                out.append(dg * u[c] - near + (gradients[c] - here))
            return consume(i, w, u, out), here

        def body(rows, before):
            stores = []
            for i in rows:
                more, before = one(i, before)
                stores += more
            for ref, index, value in stores:
                ref[index] = value
            return before

        lo = HX - halo
        uz = src[2, lo - 1, w, :]
        before = div(flat(lo - 1, w, wp), uz, roll(uz, -z))
        most = 4 if self.number == 0 else 7
        rows_loop(lo, self.xsize + 2 * halo, most, body, before)

    def step(self, src, dst, halo, number, window=None, out=None):
        rates = rate_list()

        def consume(i, w, u, au):
            gain = 1.0 / THETA if number == 0 else 2.0 * rates[number] / DELTA
            inv = gain * self.inv[i, w, :]
            stores = []
            for c in range(3):
                p = inv * (self.f[c, i, w, :] - au[c])
                if number:
                    p = p + rates[number] * rates[number - 1] * self.p[c, i, w, :]
                at = (c, i, w, slice(None))
                if number < 3:
                    stores.append((self.p, at, p))
                if out is not None:
                    stores.append((out, (c, i - HX), u[c] + p))
                else:
                    stores.append((dst, at, u[c] + p))
            return stores

        self.sweep(src, halo, window or self.window, consume)

    def first_direction(self, halo):
        w0, wn = self.window
        w = slice(w0, w0 + wn)

        def body(rows, carry):
            stores = []
            for i in rows:
                inv = (1.0 / THETA) * self.inv[i, w, :]
                stores += [(i, c, inv * self.f[c, i, w, :]) for c in range(3)]
            for i, c, p in stores:
                self.p[c, i, w, :] = p
                self.xa[c, i, w, :] = p

        rows_loop(HX - halo, self.xsize + 2 * halo, 4, body)

    def smooth_down(self, halo):
        self.step(self.xa, self.xb, max(halo - 1, 0), 1)
        self.step(self.xb, self.xa, max(halo - 2, 0), 2)
        self.step(self.xa, self.xb, max(halo - 3, 0), 3)

    def residual(self):
        def consume(i, w, u, au):
            at = [(c, i, w, slice(None)) for c in range(3)]
            return [(self.p, at[c], self.f[c, i, w, :] - au[c]) for c in range(3)]

        self.sweep(self.xb, 0, (HY, round8(self.ysize)), consume)

    def add_grown(self, coarse, xoff, yoff, temp):
        w0, wn = self.window
        w = slice(w0, w0 + wn)
        half = wn // 2
        rows = pl.ds(yoff + HY + (w0 - HY) // 2, half)

        def body(js, carry):
            for n, j in enumerate(js):
                for c in range(3):
                    value = coarse[c, j + (xoff + HX - 2), rows, :]
                    temp[3 * n + c, pl.ds(0, half, stride=2), :] = value
                    temp[3 * n + c, pl.ds(1, half, stride=2), :] = value
            for n, j in enumerate(js):
                for c in range(3):
                    grown = temp[3 * n + c, 0:wn, :]
                    for t in range(2):
                        i = HX - 4 + 2 * j + t
                        self.xa[c, i, w, :] = self.xb[c, i, w, :] + grown

        rows_loop(0, (self.xsize + 8) // 2, 4, body)


def shrink_fields(fine, pairs):
    half = fine.ysize // 2

    def body(js, carry):
        values = []
        for j in js:
            for load, store in pairs:
                total = load(2 * j, 0, half) + load(2 * j, 1, half)
                total = total + (load(2 * j + 1, 0, half) + load(2 * j + 1, 1, half))
                values.append((store, j, 0.125 * halve_lanes(total, fine.group)))
        for store, j, value in values:
            store(j, value)

    rows_loop(0, fine.xsize // 2, 4, body)


def plan(xsize, ysize, groups, bricks):
    levels = []
    for number in range(3):
        size = ysize >> number
        levels.append(Level(number, xsize >> number, size, (HY - 4, round8(size + 8))))
    coarse = (xsize >> 3) * groups, (ysize >> 3) * bricks
    levels.append(Level(3, coarse[0], coarse[1], (HY, round8(coarse[1]))))
    size = xsize
    exchanges = dict(
        c0=Exchange(size, 1, 5, (4, 5)),
        f0=Exchange(size, 1, 4, (4, 4, 4)),
        c1=Exchange(size // 2, 2, 3, (4, 5)),
        c2=Exchange(size // 4, 4, 1, (4, 4)),
        f1=Exchange(size // 2, 2, 2, (4, 4, 4)),
        f2=Exchange(size // 4, 4, 1, (4,) * 6),
        x0=Exchange(size, 1, 4, (4, 4, 4)),
        x1=Exchange(size // 2, 2, 2, (4, 4, 4)),
        x2=Exchange(size // 4, 4, 1, (4, 4, 4)),
        y2=Exchange(size // 4, 4, 1, (2, 2, 2)),
        y1=Exchange(size // 2, 2, 1, (2, 2, 2)),
    )
    return levels, exchanges


def cycle(groups, bricks, xsize, ysize, f_in, k_in, rea_in, out, *scratch):
    levels, exchanges = plan(xsize, ysize, groups, bricks)
    devices = groups * bricks
    g, b = lax.axis_index("grp"), lax.axis_index("brick")
    me = g * bricks + b
    exists = {}
    for dx, dy in DIRS:
        good = None
        for d, at, count in ((dx, g, groups), (dy, b, bricks)):
            if d:
                test = at > 0 if d < 0 else at < count - 1
                good = test if good is None else good & test
        exists[(dx, dy)] = good
    scratch = list(scratch)

    def take(count):
        got = scratch[:count]
        del scratch[:count]
        return got

    for level in levels:
        level.bind(take(12))
    for name in exchanges:
        exchanges[name].bind(take(8), (g, b, exists))
    temp, slot, slots, slot_send, slot_recv = take(5)
    ex = exchanges
    l0, l1, l2, l3 = levels

    barrier = pltpu.get_barrier_semaphore()

    def partner(n):
        other = (me + n) % devices
        return other // bricks, other % bricks

    def greet(n, carry):
        pl.semaphore_signal(
            barrier, inc=1, device_id=partner(n), device_id_type=pl.DeviceIdType.MESH
        )
        return carry

    lax.fori_loop(1, devices, greet, 0)

    def get_coeff(field, i, r0, count):
        return (rea_in, k_in)[field][i, r0 : r0 + count, :]

    def get_source(field, i, r0, count):
        return f_in[field, i, r0 : r0 + count, :]

    ex["c0"].stage(get_coeff)
    pl.semaphore_wait(barrier, devices - 1)
    ex["c0"].start()
    ex["f0"].stage(get_source)
    ex["f0"].start()

    for level in levels:
        level.clear()

    def load_own(i, carry):
        own = slice(HY, HY + ysize)
        for c in range(3):
            l0.f[c, HX + i, own, :] = f_in[c, i]
        l0.k[HX + i, own, :] = k_in[i]
        l0.rea[HX + i, own, :] = rea_in[i]
        return carry

    lax.fori_loop(0, xsize, load_own, 0)

    def shrink_pair(ref, target):
        def load(x, y, count):
            return ref[HX + x, pl.ds(HY + y, count, stride=2), :]

        def store(j, value):
            target[HX + j, HY : HY + value.shape[0], :] = value

        return load, store

    for fine, coarse in ((l0, l1), (l1, l2)):
        pairs = [shrink_pair(fine.k, coarse.k), shrink_pair(fine.rea, coarse.rea)]
        shrink_fields(fine, pairs)

    def getter(*refs):
        def get(field, i, r0, count):
            ref, c = refs[field]
            rows = slice(HY + r0, HY + r0 + count)
            return ref[HX + i, rows, :] if c is None else ref[c, HX + i, rows, :]

        return get

    def putter(*refs):
        def put(field, i, r0, value):
            ref, c = refs[field]
            rows = slice(HY + r0, HY + r0 + value.shape[0])
            if c is None:
                ref[HX + i, rows, :] = value
            else:
                ref[c, HX + i, rows, :] = value

        return put

    def three(ref):
        return tuple((ref, c) for c in range(3))

    def own_prepare(level, halo):
        xs, ys = level.xsize, level.ysize
        level.prepare(halo, g * xs, b * ys, xs * groups, ys * bricks)

    ex["c1"].stage(getter((l1.rea, None), (l1.k, None)))
    ex["c2"].stage(getter((l2.rea, None), (l2.k, None)))
    ex["c0"].finish(putter((l0.rea, None), (l0.k, None)))

    def shrink_residual(fine, coarse):
        pairs = [shrink_pair(fine.p.at[c], coarse.f.at[c]) for c in range(3)]
        shrink_fields(fine, pairs)

    own_prepare(l0, 4)
    ex["f0"].finish(putter(*three(l0.f)))
    ex["c1"].start()
    ex["c2"].start()
    l0.first_direction(4)
    l0.smooth_down(4)
    l0.residual()
    shrink_residual(l0, l1)

    ex["f1"].stage(getter(*three(l1.f)))
    ex["f1"].start()
    ex["x0"].stage(getter(*three(l0.xb)))
    ex["c1"].finish(putter((l1.rea, None), (l1.k, None)))
    ex["c2"].finish(putter((l2.rea, None), (l2.k, None)))
    own_prepare(l1, 4)
    own_prepare(l2, 4)
    ex["f1"].finish(putter(*three(l1.f)))
    l1.first_direction(4)
    l1.smooth_down(4)
    l1.residual()
    shrink_residual(l1, l2)

    l2.first_direction(0)
    ex["f2"].stage(getter(*three(l2.f), *three(l2.p)))
    ex["f2"].start()
    ex["x1"].stage(getter(*three(l1.xb)))

    def put_f2(field, i, r0, value):
        putter(*three(l2.f), *three(l2.p))(field, i, r0, value)
        if field >= 3:
            putter(*three(l2.xa))(field - 3, i, r0, value)

    for name in ("c0", "f0", "c1", "c2", "f1"):
        ex[name].finish_send()
    ex["f2"].finish(put_f2)
    l2.smooth_down(4)
    ex["x2"].stage(getter(*three(l2.xb)))
    ex["x2"].start()
    l2.residual()

    def load_fine(field, x, y):
        rows = slice(HY + y, HY + y + 1)
        if field < 3:
            return l2.p[field, HX + x, rows, :]
        return (l2.rea if field == 3 else l2.k)[HX + x, rows, :]

    slot[...] = jnp.zeros_like(slot)
    for field in range(5):
        values = []
        for x in range(2):
            for y in range(2):
                total = load_fine(field, 2 * x, 2 * y) + load_fine(field, 2 * x, 2 * y + 1)
                total = total + load_fine(field, 2 * x + 1, 2 * y)
                total = total + load_fine(field, 2 * x + 1, 2 * y + 1)
                values.append(0.125 * halve_lanes(total, 4))
        slot[field : field + 1, :] = pack(values, 8)

    def gather_copy(n):
        return pltpu.make_async_remote_copy(
            src_ref=slot,
            dst_ref=slots.at[pl.ds(me * 8, 8)],
            send_sem=slot_send.at[n],
            recv_sem=slot_recv.at[me],
            device_id=partner(n),
            device_id_type=pl.DeviceIdType.MESH,
        )

    def send_slot(n, carry):
        gather_copy(n).start()
        return carry

    lax.fori_loop(1, devices, send_slot, 0)

    slots[pl.ds(pl.multiple_of(me * 8, 8), 8), :] = slot[...]

    def receive(n, carry):
        owner = (me + n) % devices
        pltpu.make_async_remote_copy(
            src_ref=slot,
            dst_ref=slots.at[pl.ds(owner * 8, 8)],
            send_sem=slot_send.at[n],
            recv_sem=slot_recv.at[owner],
            device_id=partner(n),
            device_id_type=pl.DeviceIdType.MESH,
        ).wait_recv()
        return carry

    lax.fori_loop(1, devices, receive, 0)
    ex["x1"].start()
    ex["x0"].start()
    for og in range(groups):
        for field in range(5):
            value = slots[pl.ds(og * bricks * 8 + field, bricks, stride=8), :]
            for x in range(2):
                for y in range(2):
                    line = unpack(value, 8, 2 * x + y)
                    row, cols = HX + 2 * og + x, pl.ds(HY + y, bricks, stride=2)
                    if field < 3:
                        l3.f[field, row, cols, :] = line
                    else:
                        (l3.rea if field == 3 else l3.k)[row, cols, :] = line
    l3.prepare(0, 0, 0, l3.xsize, l3.ysize)
    edge = slice(l3.window[0], l3.window[0] + l3.window[1])
    l3.kx[HX - 1, edge, :] = (0.5 * l3.scale) * l3.k[HX, edge, :]
    l3.first_direction(0)
    l3.smooth_down(0)

    ex["x2"].finish(putter(*three(l2.xb)))
    l2.add_grown(l3.xb, g * (xsize // 8), b * (ysize // 8), temp)
    up(l2)
    ex["y2"].stage(getter(*three(l2.xa)))
    ex["y2"].start()
    ex["x1"].finish(putter(*three(l1.xb)))

    def sent(n, carry):
        gather_copy(n).wait_send()
        return carry

    lax.fori_loop(1, devices, sent, 0)
    for name in ("f2", "x1", "x2"):
        ex[name].finish_send()
    ex["y2"].finish(putter(*three(l2.xa)))
    l1.add_grown(l2.xa, 0, 0, temp)
    up(l1)
    ex["y1"].stage(getter(*three(l1.xa)))
    ex["y1"].start()
    ex["x0"].finish(putter(*three(l0.xb)))
    ex["y2"].finish_send()
    ex["y1"].finish(putter(*three(l1.xa)))
    l0.add_grown(l1.xa, 0, 0, temp)
    up(l0, out)

    ex["x0"].finish_send()
    ex["y1"].finish_send()


def up(level, out=None):
    level.step(level.xa, level.xb, 3, 0)
    level.step(level.xb, level.xa, 2, 1)
    level.step(level.xa, level.xb, 1, 2)
    level.step(level.xb, level.xa, 0, 3, (HY, round8(level.ysize)), out)


def on_device(right_side, stiffness, reaction):
    groups, bricks = lax.axis_size("grp"), lax.axis_size("brick")
    _, xsize, ysize, _ = right_side.shape
    levels, exchanges = plan(xsize, ysize, groups, bricks)
    devices = groups * bricks
    scratch = []
    for level in levels:
        scratch += level.scratch()
    for name in exchanges:
        scratch += exchanges[name].scratch()
    scratch += [
        pltpu.VMEM((12, 32, LANES), jnp.float32),
        pltpu.VMEM((8, LANES), jnp.float32),
        pltpu.VMEM((8 * devices, LANES), jnp.float32),
        pltpu.SemaphoreType.DMA((devices,)),
        pltpu.SemaphoreType.DMA((devices,)),
    ]

    def kernel(*refs):
        cycle(groups, bricks, xsize, ysize, *refs)

    vmem = pl.BlockSpec(memory_space=pltpu.VMEM)
    return pl.pallas_call(
        kernel,
        out_shape=jax.ShapeDtypeStruct(right_side.shape, jnp.float32),
        in_specs=[vmem] * 3,
        out_specs=vmem,
        scratch_shapes=scratch,
        compiler_params=pltpu.CompilerParams(
            collective_id=0, has_side_effects=True, vmem_limit_bytes=56 * 2**20
        ),
    )(right_side, stiffness, reaction)


def solution(mesh):
    in_specs = (P(None, "grp", "brick", None), P("grp", "brick", None), P("grp", "brick", None))
    out_specs = P(None, "grp", "brick", None)
    return jax.shard_map(
        on_device, mesh=mesh, in_specs=in_specs, out_specs=out_specs, check_vma=False
    )
```
